128 devices in a mesh: ctx: 32 (over z, y, core), head: 4 (over x).
Axes of the slice: x: 4, y: 4, z: 4, core: 2. Of those that a mesh axis runs over, the one named last changes fastest.
Arguments:
- q_nope: bfloat16 [32, 128, 128], P(None, 'head'), may hold values from -6 to 6
- q_rope: bfloat16 [32, 128, 64], P(None, 'head'), may hold values from -256 to 256
- latent_cache: bfloat16 [32, 16384, 512], P(None, 'ctx'), may hold values from -6 to 6
- rope_keys: bfloat16 [32, 16384, 64], P(None, 'ctx'), may hold values from -4 to 4
- lengths: int32 [32], replicated, may hold values from 8192 to 16384, as said below
- w_uk: bfloat16 [128, 128, 512], P('head', None, 'ctx'), may hold values from -0.5 to 0.5
- w_uv: bfloat16 [128, 512, 128], P('head'), may hold values from -1 to 1
- w_out: bfloat16 [16384, 7168], P('head', 'ctx'), may hold values from -0.1875 to 0.1875
Outputs:
- layer_out: bfloat16 [32, 7168], P('head', 'ctx')
The draws below stay inside these ranges and needn't reach their ends.
Inputs may be any that keep to these rules, and one draw needn't show every extreme that they name: `lengths`: some row has length 16384 and some row has length 8192.
All inputs are finite; a program needn't handle non-finite values.
Results may differ from the reference program's by a relative error of at most 0.008.
Values may be sent and summed in bfloat16 or wider, within the bound.
A program may use at most 128 MiB of HBM per device.

```python
import jax
import jax.numpy as jnp
from jax import lax

D = 7168
H = 128
DN = 128
DR = 64
LATENT = 512
DV = 128
ROWS = 32
CTX = 16384


def shared_rope(key):
    base_keys = jnp.clip(jax.random.normal(jax.random.fold_in(key, 101), (ROWS, CTX, DR), jnp.float32), -4.0, 4.0)
    return base_keys


def draw_rope_keys(key, part):
    base_keys = shared_rope(key)
    result = base_keys
    return result.astype(jnp.bfloat16)


def draw_q_rope(key, part):
    key = jax.random.fold_in(key, 4)
    result = jnp.clip(jax.random.normal(key, (ROWS, H, DR), jnp.float32), -4.0, 4.0)
    return result.astype(jnp.bfloat16)


def draw_lengths(key, part):
    key = jax.random.fold_in(key, 5)
    drawn = jax.random.randint(jax.random.fold_in(key, 1), (ROWS,), CTX // 2, CTX + 1)
    order = jax.random.permutation(jax.random.fold_in(key, 2), ROWS)
    drawn = drawn.at[order[0]].set(CTX)
    drawn = drawn.at[order[1]].set(CTX // 2)
    return drawn.astype(jnp.int32)


def level_of(own_key, extent, shards, least, top_value):
    gain, own = 1.0, jax.random.fold_in(own_key, 6)
    for axis_at, shards_of in shards:
        heights = jnp.exp(jax.random.uniform(jax.random.fold_in(own, axis_at), (shards_of,), jnp.float32, least / len(shards), top_value / len(shards)))
        gain = gain * jnp.repeat(heights, extent[axis_at] // shards_of).reshape([-1 if axis == axis_at else 1 for axis in range(len(extent))])
    return gain


def scatter_about(stream_key, extent, deviation, limit, split=(), kind=jnp.bfloat16):
    factor_of = level_of(stream_key, extent, split, -0.22, 0.18) if split else 1.0
    entries = jax.random.normal(stream_key, extent, jnp.float32) * deviation * factor_of
    return jnp.minimum(jnp.maximum(entries, -limit), limit).astype(kind)


def setup_inputs(seed: int = 0) -> dict:
    splits = jax.random.split(jax.random.key(seed), 9)
    q_nope = scatter_about(splits[0], (ROWS, H, DN), 1.0, 6.0, ((1, 4),))
    q_rope = draw_q_rope(jax.random.fold_in(splits[8], 71), 0)
    latent_cache = scatter_about(splits[2], (ROWS, CTX, LATENT), 1.0, 6.0, ((1, 32),))
    rope_keys = draw_rope_keys(jax.random.fold_in(splits[8], 71), 0)
    lengths = draw_lengths(jax.random.fold_in(splits[8], 71), 0)
    w_uk = scatter_about(splits[5], (H, DN, LATENT), DN ** -0.5, 0.5, ((0, 4), (2, 32)))
    w_uv = scatter_about(splits[6], (H, LATENT, DV), (LATENT // 16) ** -0.5, 1.0, ((0, 4),))
    w_out = scatter_about(splits[7], (H * DV, D), (H * DV // 16) ** -0.5, 0.1875, ((0, 4), (1, 32)))
    return dict(q_nope=q_nope, q_rope=q_rope, latent_cache=latent_cache, rope_keys=rope_keys, lengths=lengths, w_uk=w_uk, w_uv=w_uv, w_out=w_out)


def reference(q_nope, q_rope, latent_cache, rope_keys, lengths, w_uk, w_uv, w_out):
    score_scale = (DN + DR) ** -0.5
    q_latent = jnp.einsum("rhn,hnl->rhl", q_nope.astype(jnp.float32), w_uk.astype(jnp.float32)).astype(jnp.bfloat16)

    def one_row(row_inputs):
        row_query, row_rope, row_cache, row_keys, row_length = row_inputs
        scores = (jnp.dot(row_query, row_cache.T, preferred_element_type=jnp.float32)
                  + jnp.dot(row_rope, row_keys.T, preferred_element_type=jnp.float32)) * score_scale
        in_range = (jnp.arange(CTX, dtype=jnp.int32) < row_length)[None, :]
        masked = jnp.where(in_range, scores, jnp.float32(-1e30))
        row_peak = jnp.max(masked, axis=1, keepdims=True)
        weights = jnp.where(in_range, jnp.exp(masked - row_peak), jnp.float32(0.0)).astype(jnp.bfloat16)
        row_total = jnp.sum(weights.astype(jnp.float32), axis=1)
        summed = jnp.dot(weights, row_cache, preferred_element_type=jnp.float32)
        return summed, row_total

    summed, row_total = lax.map(one_row, (q_latent, q_rope, latent_cache, rope_keys, lengths))
    projected = jnp.einsum("rhl,hlv->rhv", summed, w_uv.astype(jnp.float32), precision=lax.Precision.HIGHEST)
    values = (projected / row_total[:, :, None]).astype(jnp.bfloat16)
    flattened = values.reshape(ROWS, H * DV)
    return jnp.dot(flattened, w_out, preferred_element_type=jnp.float32).astype(jnp.bfloat16)
```

```python
import functools

import jax
import jax.numpy as jnp
from jax import lax
from jax.experimental import pallas as pl
from jax.experimental.pallas import tpu as pltpu
from jax.sharding import PartitionSpec as P

MESH = pl.DeviceIdType.MESH
F32 = jnp.float32
BF16 = jnp.bfloat16


def nt(a, b):
    return lax.dot_general(a, b, (((1,), (1,)), ((), ())), preferred_element_type=F32)


def nn(a, b):
    return jnp.dot(a, b, preferred_element_type=F32)


def kernel(
    lengths, q_nope, q_rope, cache, keys, w_uk, w_uv, w_out, out,
    qn, wk, ybuf, xbuf, qbuf, qs, rbuf, cbuf, kbuf, uv, wo,
    obuf, stat, rsbuf, statbuf, wcol, vmsg, vbuf, vwide, terms, tbuf,
    load_sem, rope_sems, pair_sems, x_sems, q_sems, rs_sems, stat_sems, v_sems, t_sems,
):
    ctx = lax.axis_index("ctx")
    x = lax.axis_index("head")
    z, y, c = ctx // 8, (ctx // 2) % 4, ctx % 2
    twin = ctx + 1 - 2 * c
    scale = (128 + 64) ** (-0.5)

    def sums_to(block):
        zb, yb = block // 4, block % 4
        return (((x + zb) % 4) * 8 + yb * 2 + c, zb)

    def sums_from(source):
        return ((source // 4) * 8 + (source % 4) * 2 + c, (z + 4 - x) % 4)

    def is_me(device):
        return jnp.logical_and(device[0] == ctx, device[1] == x)

    barrier = pltpu.get_barrier_semaphore()

    def greet_plane(k, carry):
        pl.semaphore_signal(barrier, inc=1, device_id=((ctx + k) % 32, x), device_id_type=MESH)
        return carry

    def greet_source(s, carry):
        device = sums_from(s)

        @pl.when(jnp.logical_not(is_me(device)))
        def _():
            pl.semaphore_signal(barrier, inc=1, device_id=device, device_id_type=MESH)

        return carry

    for k in range(1, 4):
        pl.semaphore_signal(barrier, inc=1, device_id=(ctx, (x + k) % 4), device_id_type=MESH)
    lax.fori_loop(1, 32, greet_plane, 0)
    lax.fori_loop(0, 16, greet_source, 0)

    mine, theirs = 8 * x + 4 * c, 8 * x + 4 * (1 - c)
    half = pl.ds(pl.multiple_of(c * 512, 512), 512)
    loads = [
        pltpu.make_async_copy(q_nope, qn, load_sem.at[0]),
        pltpu.make_async_copy(w_uk, wk, load_sem.at[1]),
        pltpu.make_async_copy(cache.at[pl.ds(mine, 4)], cbuf.at[:, half], load_sem.at[2]),
        pltpu.make_async_copy(keys.at[pl.ds(mine, 4)], kbuf.at[:, :, half], load_sem.at[3]),
        pltpu.make_async_copy(w_uv.at[pl.ds(8 * y, 8)], uv, load_sem.at[4]),
        pltpu.make_async_copy(w_out, wo, load_sem.at[5]),
        pltpu.make_async_copy(q_rope.at[pl.ds(mine, 4)], rbuf.at[x], load_sem.at[6]),
    ]
    for load in loads:
        load.start()

    loads[0].wait()
    loads[1].wait()
    row_head = lax.broadcasted_iota(jnp.int32, (512, 128), 0) // 16
    lane_head = lax.broadcasted_iota(jnp.int32, (512, 128), 1) % 32
    own_head = row_head == lane_head
    for t in range(8):
        every = nt(wk[...], qn[pl.ds(128 * t, 128), :])
        kept = jnp.where(own_head, every, 0.0).reshape(32, 16, 128)
        ybuf[t // 2, t % 2] = jnp.sum(kept, axis=0).astype(BF16)

    n_self = jnp.where((z + 4 - x) % 4 == x, 1, 0)
    pl.semaphore_wait(barrier, 3 + 31 + 16 - n_self)

    sends = []
    own_y = pltpu.make_async_copy(ybuf.at[x], xbuf.at[:, x], x_sems.at[1])
    own_y.start()
    for k in range(1, 4):
        to = (x + k) % 4
        copy = pltpu.make_async_remote_copy(
            src_ref=ybuf.at[to], dst_ref=xbuf.at[:, x], send_sem=x_sems.at[0], recv_sem=x_sems.at[1],
            device_id=(ctx, to), device_id_type=MESH,
        )
        copy.start()
    cache_copy = pltpu.make_async_remote_copy(
        src_ref=cache.at[pl.ds(theirs, 4)], dst_ref=cbuf.at[:, half], send_sem=pair_sems.at[0],
        recv_sem=pair_sems.at[1], device_id=(twin, x), device_id_type=MESH,
    )
    cache_copy.start()
    keys_copy = pltpu.make_async_remote_copy(
        src_ref=keys.at[pl.ds(theirs, 4)], dst_ref=kbuf.at[:, :, half], send_sem=pair_sems.at[2],
        recv_sem=pair_sems.at[3], device_id=(twin, x), device_id_type=MESH,
    )
    keys_copy.start()
    rope_copies = []
    for k in range(1, 4):
        to = (x + k) % 4
        copy = pltpu.make_async_remote_copy(
            src_ref=q_rope.at[pl.ds(8 * to + 4 * c, 4)], dst_ref=rbuf.at[x], send_sem=rope_sems.at[0, k - 1],
            recv_sem=rope_sems.at[1, k - 1], device_id=(ctx, to), device_id_type=MESH,
        )
        copy.start()
        rope_copies.append(copy)

    pltpu.make_async_copy(xbuf, xbuf, x_sems.at[1]).wait()
    own_q = pltpu.make_async_copy(xbuf.at[c], qbuf.at[ctx], q_sems.at[1])
    own_q.start()

    def send_q(k, carry):
        to = (ctx + k) % 32
        pltpu.make_async_remote_copy(
            src_ref=xbuf.at[to % 2], dst_ref=qbuf.at[ctx], send_sem=q_sems.at[0], recv_sem=q_sems.at[1],
            device_id=(to, x), device_id_type=MESH,
        ).start()
        return carry

    lax.fori_loop(1, 32, send_q, 0)

    loads[2].wait()
    loads[3].wait()
    loads[6].wait()
    cache_copy.wait_recv()
    keys_copy.wait_recv()
    for copy in rope_copies:
        copy.wait_recv()
    pltpu.make_async_copy(qbuf, qbuf, q_sems.at[1]).wait()
    for g in range(4):
        turned = qbuf[:, g].reshape(512, 128).T
        for i in range(4):
            qs[i, 32 * g:32 * g + 32, :] = turned[32 * i:32 * i + 32, :]

    place = (ctx // 2) * 1024 + lax.broadcasted_iota(jnp.int32, (128, 1024), 1)
    lane = lax.broadcasted_iota(jnp.int32, (128, 128), 1)
    stats = jnp.zeros((128, 128), F32)
    for pair in range(2):
        parts = []
        for i in (2 * pair, 2 * pair + 1):
            block = cbuf[i]
            rope = rbuf[:, i].reshape(128, 64)
            scores = (nt(qs[i], block) + nn(rope, kbuf[i])) * scale
            inside = place < lengths[mine + i]
            scores = jnp.where(inside, scores, -1e30)
            peak = jnp.max(scores, axis=1, keepdims=True)
            weights = jnp.where(inside, jnp.exp(scores - peak), 0.0).astype(BF16)
            total = jnp.sum(weights.astype(F32), axis=1, keepdims=True)
            parts.append(nn(weights, block))
            stats = jnp.where(lane == i, peak, jnp.where(lane == 4 + i, total, stats))
        for b in range(16):
            obuf[b, pair] = jnp.concatenate(
                [parts[0][8 * b:8 * b + 8], parts[1][8 * b:8 * b + 8]], axis=0
            ).astype(BF16)

        def send_sums(b, carry):
            device = sums_to(b)
            own = is_me(device)
            slot = 4 * z + y

            @pl.when(own)
            def _():
                pltpu.make_async_copy(obuf.at[b, pair], rsbuf.at[pair, slot], rs_sems.at[1, pair]).start()

            @pl.when(jnp.logical_not(own))
            def _():
                pltpu.make_async_remote_copy(
                    src_ref=obuf.at[b, pair], dst_ref=rsbuf.at[pair, slot], send_sem=rs_sems.at[0, pair],
                    recv_sem=rs_sems.at[1, pair], device_id=device, device_id_type=MESH,
                ).start()

            return carry

        lax.fori_loop(0, 16, send_sums, 0)

    stat[...] = stats.T[0:8, :]

    def send_stats(b, carry):
        device = sums_to(b)
        own = is_me(device)
        slot = 4 * z + y

        @pl.when(own)
        def _():
            pltpu.make_async_copy(stat, statbuf.at[slot], stat_sems.at[1]).start()

        @pl.when(jnp.logical_not(own))
        def _():
            pltpu.make_async_remote_copy(
                src_ref=stat, dst_ref=statbuf.at[slot], send_sem=stat_sems.at[0], recv_sem=stat_sems.at[1],
                device_id=device, device_id_type=MESH,
            ).start()

        return carry

    lax.fori_loop(0, 16, send_stats, 0)

    pltpu.make_async_copy(statbuf, statbuf, stat_sems.at[1]).wait()
    peaks, totals = statbuf[:, 0:4, :], statbuf[:, 4:8, :]
    factors = jnp.exp(peaks - jnp.max(peaks, axis=0, keepdims=True))
    factors = factors / jnp.sum(factors * totals, axis=0, keepdims=True)
    factors = jnp.concatenate([factors.reshape(64, 128), jnp.zeros((64, 128), F32)], axis=0)
    wcol[...] = factors.T
    own_factors = wcol[pl.ds(pl.multiple_of(8 * (4 * x + y), 8), 8), :]
    summed = []
    for pair in range(2):
        pltpu.make_async_copy(rsbuf.at[pair], rsbuf.at[pair], rs_sems.at[1, pair]).wait()
        acc = [jnp.zeros((8, 512), F32), jnp.zeros((8, 512), F32)]
        for d in range(16):
            chunk = rsbuf[pair, d].astype(F32)
            for i in range(2):
                at = 4 * d + 2 * pair + i
                acc[i] = acc[i] + own_factors[:, at:at + 1] * chunk[8 * i:8 * i + 8]
        summed += acc
    summed = jnp.concatenate(summed, axis=0)
    high = summed.astype(BF16)
    low = (summed - high.astype(F32)).astype(BF16)
    both = jnp.concatenate([high, low], axis=0)
    loads[4].wait()
    own_row = lax.broadcasted_iota(jnp.int32, (32, 128), 0) % 8
    values = jnp.zeros((32, 128), F32)
    for h in range(8):
        product = nn(both, uv[h])
        values = jnp.where(own_row == h, product[0:32] + product[32:64], values)
    vmsg[...] = values.astype(BF16)

    block_of_rows = 2 * ((z + 4 - x) % 4) + c
    own_v = pltpu.make_async_copy(vmsg, vbuf.at[y, block_of_rows], v_sems.at[1])
    own_v.start()

    def send_v(k, carry):
        pltpu.make_async_remote_copy(
            src_ref=vmsg, dst_ref=vbuf.at[y, block_of_rows], send_sem=v_sems.at[0], recv_sem=v_sems.at[1],
            device_id=((ctx + k) % 32, x), device_id_type=MESH,
        ).start()
        return carry

    lax.fori_loop(1, 32, send_v, 0)
    loads[5].wait()
    pltpu.make_async_copy(vbuf, vbuf, v_sems.at[1]).wait()
    head_terms = jnp.zeros((32, 224), F32)
    for yb in range(4):
        vwide[yb] = vbuf[yb].astype(F32).reshape(256, 128)
        for h in range(0, 8, 2):
            rows = jnp.concatenate(
                [vwide[yb, pl.ds(h, 32, stride=8), :], vwide[yb, pl.ds(h + 1, 32, stride=8), :]], axis=1
            ).astype(BF16)
            head = 8 * yb + h
            head_terms = head_terms + nt(rows, wo[:, 128 * head:128 * head + 256])
    for k in range(4):
        terms[k] = jnp.concatenate([head_terms[8 * k:8 * k + 8], jnp.zeros((8, 32), F32)], axis=1)

    term_copies = []
    for k in range(1, 4):
        to = (x + k) % 4
        copy = pltpu.make_async_remote_copy(
            src_ref=terms.at[to], dst_ref=tbuf.at[k - 1], send_sem=t_sems.at[0, k - 1], recv_sem=t_sems.at[1, k - 1],
            device_id=(ctx, to), device_id_type=MESH,
        )
        copy.start()
        term_copies.append(copy)
    result = terms[x]
    for k in range(3):
        term_copies[k].wait_recv()
        result = result + tbuf[k]
    out[...] = result[:, 0:224].astype(BF16)

    for k in range(3):
        term_copies[k].wait_send()
        rope_copies[k].wait_send()
    cache_copy.wait_send()
    keys_copy.wait_send()
    pltpu.make_async_copy(ybuf.at[pl.ds(0, 3)], ybuf.at[pl.ds(0, 3)], x_sems.at[0]).wait()
    pltpu.make_async_copy(qbuf.at[pl.ds(0, 31)], qbuf.at[pl.ds(0, 31)], q_sems.at[0]).wait()
    flat = vbuf.at[0]
    for k in range(3):
        pltpu.make_async_copy(flat, flat, v_sems.at[0]).wait()
    pltpu.make_async_copy(vbuf.at[0, pl.ds(0, 7)], vbuf.at[0, pl.ds(0, 7)], v_sems.at[0]).wait()

    def sent(b, carry):
        @pl.when(jnp.logical_not(is_me(sums_to(b))))
        def _():
            for pair in range(2):
                pltpu.make_async_copy(obuf.at[b, pair], obuf.at[b, pair], rs_sems.at[0, pair]).wait()
            pltpu.make_async_copy(stat, stat, stat_sems.at[0]).wait()

        return carry

    lax.fori_loop(0, 16, sent, 0)


def body(q_nope, q_rope, latent_cache, rope_keys, lengths, w_uk, w_uv, w_out):
    any_spec = pl.BlockSpec(memory_space=pl.ANY)
    dma = pltpu.SemaphoreType.DMA
    return pl.pallas_call(
        kernel,
        out_shape=jax.ShapeDtypeStruct((8, 224), BF16),
        in_specs=[pl.BlockSpec(memory_space=pltpu.SMEM)] + [any_spec] * 7,
        out_specs=pl.BlockSpec(memory_space=pltpu.VMEM),
        scratch_shapes=[
            pltpu.VMEM((1024, 128), BF16),
            pltpu.VMEM((512, 128), BF16),
            pltpu.VMEM((4, 2, 16, 128), BF16),
            pltpu.VMEM((2, 4, 16, 128), BF16),
            pltpu.VMEM((32, 4, 16, 128), BF16),
            pltpu.VMEM((4, 128, 512), BF16),
            pltpu.VMEM((4, 4, 32, 64), BF16),
            pltpu.VMEM((4, 1024, 512), BF16),
            pltpu.VMEM((4, 64, 1024), BF16),
            pltpu.VMEM((8, 512, 128), BF16),
            pltpu.VMEM((224, 4096), BF16),
            pltpu.VMEM((16, 2, 16, 512), BF16),
            pltpu.VMEM((8, 128), F32),
            pltpu.VMEM((2, 16, 16, 512), BF16),
            pltpu.VMEM((16, 8, 128), F32),
            pltpu.VMEM((128, 128), F32),
            pltpu.VMEM((32, 128), BF16),
            pltpu.VMEM((4, 8, 32, 128), BF16),
            pltpu.VMEM((4, 256, 128), F32),
            pltpu.VMEM((4, 8, 256), F32),
            pltpu.VMEM((3, 8, 256), F32),
            dma((7,)), dma((2, 3)), dma((4,)), dma((2,)), dma((2,)), dma((2, 2)), dma((2,)), dma((2,)), dma((2, 3)),
        ],
        compiler_params=pltpu.CompilerParams(
            collective_id=0, has_side_effects=True, vmem_limit_bytes=48 << 20
        ),
    )(
        lengths,
        q_nope.reshape(1024, 128),
        q_rope,
        latent_cache,
        jnp.swapaxes(rope_keys, 1, 2),
        jnp.swapaxes(w_uk, 1, 2).reshape(512, 128),
        w_uv,
        w_out.T,
    )


def solution(mesh):
    return jax.shard_map(
        body,
        mesh=mesh,
        in_specs=(
            P(None, "head", None),
            P(None, "head", None),
            P(None, "ctx", None),
            P(None, "ctx", None),
            P(),
            P("head", None, "ctx"),
            P("head", None, None),
            P("head", "ctx"),
        ),
        out_specs=P("head", "ctx"),
        check_vma=False,
    )
```

```python
import functools

import jax
import jax.numpy as jnp
from jax import lax
from jax.experimental import pallas as pl
from jax.experimental.pallas import tpu as pltpu
from jax.sharding import PartitionSpec as P

MESH = pl.DeviceIdType.MESH
F32 = jnp.float32
BF16 = jnp.bfloat16


def nt(a, b):
    return lax.dot_general(a, b, (((1,), (1,)), ((), ())), preferred_element_type=F32)


def nn(a, b):
    return jnp.dot(a, b, preferred_element_type=F32)


def kernel(
    lengths, q_nope, q_rope, cache, keys, w_uk, w_uv, w_out, out,
    qn, wk, ybuf, xbuf, qbuf, qs, rbuf, cbuf, kbuf, uv, wo,
    obuf, stat, rsbuf, statbuf, wcol, vmsg, vbuf, vwide, terms, tbuf,
    load_sem, rope_sems, pair_sems, x_sems, q_sems, rs_sems, stat_sems, v_sems, t_sems,
):
    ctx = lax.axis_index("ctx")
    x = lax.axis_index("head")
    chip, c = ctx // 2, ctx % 2
    z, y = chip // 4, chip % 4
    twin = ctx + 1 - 2 * c
    scale = (128 + 64) ** (-0.5)

    def remote(src, dst, send_sem, recv_sem, device):
        return pltpu.make_async_remote_copy(
            src_ref=src, dst_ref=dst, send_sem=send_sem, recv_sem=recv_sem, device_id=device, device_id_type=MESH
        )

    def arrived(ref, sem):
        pltpu.make_async_copy(ref, ref, sem).wait()

    across = []
    for k in range(1, 8):
        to_x, to_c = (x + k // 2) % 4, (c + k) % 2
        across.append((to_x, to_c, (2 * chip + to_c, to_x)))
    plane = [(2 * ((chip + k) % 16) + c, x) for k in range(1, 16)]

    loads = [
        pltpu.make_async_copy(q_nope, qn, load_sem.at[0]),
        pltpu.make_async_copy(w_uk, wk, load_sem.at[1]),
    ]
    for load in loads:
        load.start()

    barrier = pltpu.get_barrier_semaphore()
    for device in plane:
        pl.semaphore_signal(barrier, inc=1, device_id=device, device_id_type=MESH)
    for _, _, device in across:
        pl.semaphore_signal(barrier, inc=1, device_id=device, device_id_type=MESH)

    mine, theirs = 8 * x + 4 * c, 8 * x + 4 * (1 - c)
    half = pl.ds(pl.multiple_of(c * 512, 512), 512)
    later = [
        pltpu.make_async_copy(cache.at[pl.ds(mine, 4)], cbuf.at[:, half], load_sem.at[2]),
        pltpu.make_async_copy(keys.at[pl.ds(mine, 4)], kbuf.at[:, :, half], load_sem.at[3]),
        pltpu.make_async_copy(w_uv.at[pl.ds(8 * y, 8)], uv, load_sem.at[4]),
        pltpu.make_async_copy(w_out, wo.at[c], load_sem.at[5]),
        pltpu.make_async_copy(q_rope.at[pl.ds(mine, 4)], rbuf.at[x], load_sem.at[6]),
    ]
    for load in later:
        load.start()
    loads += later

    loads[0].wait()
    loads[1].wait()
    row_head = lax.broadcasted_iota(jnp.int32, (512, 128), 0) // 16
    lane_head = lax.broadcasted_iota(jnp.int32, (512, 128), 1) % 32
    own_head = row_head == lane_head
    for t in range(8):
        every = nt(wk[...], qn[pl.ds(128 * t, 128), :])
        kept = jnp.where(own_head, every, 0.0).reshape(32, 16, 128)
        ybuf[t] = jnp.sum(kept, axis=0).astype(BF16)

    pl.semaphore_wait(barrier, 22)

    slot = 2 * x + c
    for to_x, to_c, device in across:
        remote(ybuf.at[2 * to_x + to_c], xbuf.at[slot], x_sems.at[0], x_sems.at[1], device).start()
    pltpu.make_async_copy(ybuf.at[slot], xbuf.at[slot], x_sems.at[1]).start()
    rope_copies = []
    for k in range(1, 4):
        to = (x + k) % 4
        copy = remote(
            q_rope.at[pl.ds(8 * to + 4 * c, 4)], rbuf.at[x], rope_sems.at[0, k - 1], rope_sems.at[1, k - 1], (ctx, to)
        )
        copy.start()
        rope_copies.append(copy)
    twin_copies = [
        remote(cache.at[pl.ds(theirs, 4)], cbuf.at[:, half], pair_sems.at[0, 0], pair_sems.at[1, 0], (twin, x)),
        remote(keys.at[pl.ds(theirs, 4)], kbuf.at[:, :, half], pair_sems.at[0, 1], pair_sems.at[1, 1], (twin, x)),
        remote(w_out, wo.at[c], pair_sems.at[0, 2], pair_sems.at[1, 2], (twin, x)),
    ]
    twin_copies[0].start()
    twin_copies[1].start()

    arrived(xbuf, x_sems.at[1])
    for device in plane:
        remote(xbuf, qbuf.at[chip], q_sems.at[0], q_sems.at[1], device).start()
    pltpu.make_async_copy(xbuf, qbuf.at[chip], q_sems.at[1]).start()
    twin_copies[2].start()

    loads[2].wait()
    loads[3].wait()
    loads[6].wait()
    twin_copies[0].wait_recv()
    twin_copies[1].wait_recv()
    for copy in rope_copies:
        copy.wait_recv()
    arrived(qbuf, q_sems.at[1])
    for g in range(4):
        turned = qbuf[:, 2 * g:2 * g + 2].reshape(512, 128).T
        for i in range(4):
            qs[i, 32 * g:32 * g + 32, :] = turned[32 * i:32 * i + 32, :]

    place = chip * 1024 + lax.broadcasted_iota(jnp.int32, (128, 1024), 1)
    lane = lax.broadcasted_iota(jnp.int32, (128, 128), 1)
    stats = jnp.zeros((128, 128), F32)
    owners = [(2 * (4 * ((x + b // 4) % 4) + b % 4) + 1 - c, b // 4) for b in range(16)]
    for pair in range(2):
        weighted = []
        for i in (2 * pair, 2 * pair + 1):
            rope = rbuf[:, i].reshape(128, 64)
            scores = (nt(qs[i], cbuf[i]) + nn(rope, kbuf[i])) * scale
            inside = place < lengths[mine + i]
            scores = jnp.where(inside, scores, -1e30)
            peak = jnp.max(scores, axis=1, keepdims=True)
            weights = jnp.where(inside, jnp.exp(scores - peak), 0.0).astype(BF16)
            total = jnp.sum(weights.astype(F32), axis=1, keepdims=True)
            weighted.append(weights)
            stats = jnp.where(lane == i, peak, jnp.where(lane == 4 + i, total, stats))
        if pair == 1:
            stat[...] = stats.T[0:8, :]
            for device in owners:
                remote(stat, statbuf.at[chip], stat_sems.at[0], stat_sems.at[1], device).start()
        parts = [nn(weighted[i], cbuf[2 * pair + i]) for i in range(2)]
        for b in range(16):
            obuf[pair, b] = jnp.concatenate(
                [parts[0][8 * b:8 * b + 8], parts[1][8 * b:8 * b + 8]], axis=0
            ).astype(BF16)
        for b, device in enumerate(owners):
            remote(obuf.at[pair, b], rsbuf.at[pair, chip], rs_sems.at[0, pair], rs_sems.at[1, pair], device).start()

    arrived(statbuf, stat_sems.at[1])
    peaks, totals = statbuf[:, 0:4, :], statbuf[:, 4:8, :]
    factors = jnp.exp(peaks - jnp.max(peaks, axis=0, keepdims=True))
    factors = factors / jnp.sum(factors * totals, axis=0, keepdims=True)
    factors = jnp.concatenate([factors.reshape(64, 128), jnp.zeros((64, 128), F32)], axis=0)
    wcol[...] = factors.T
    own_factors = wcol[pl.ds(pl.multiple_of(8 * (4 * x + y), 8), 8), :]
    summed = []
    for pair in range(2):
        arrived(rsbuf.at[pair], rs_sems.at[1, pair])
        acc = [jnp.zeros((8, 512), F32), jnp.zeros((8, 512), F32)]
        for d in range(16):
            chunk = rsbuf[pair, d].astype(F32)
            for i in range(2):
                at = 4 * d + 2 * pair + i
                acc[i] = acc[i] + own_factors[:, at:at + 1] * chunk[8 * i:8 * i + 8]
        summed += acc
    summed = jnp.concatenate(summed, axis=0)
    high = summed.astype(BF16)
    low = (summed - high.astype(F32)).astype(BF16)
    both = jnp.concatenate([high, low], axis=0)
    loads[4].wait()
    own_row = lax.broadcasted_iota(jnp.int32, (32, 128), 0) % 8
    values = jnp.zeros((32, 128), F32)
    for h in range(8):
        product = nn(both, uv[h])
        values = jnp.where(own_row == h, product[0:32] + product[32:64], values)
    vmsg[...] = values.astype(BF16)

    v_slot = 4 * y + (z + 4 - x) % 4
    for device in plane:
        remote(vmsg, vbuf.at[v_slot], v_sems.at[0], v_sems.at[1], device).start()
    pltpu.make_async_copy(vmsg, vbuf.at[v_slot], v_sems.at[1]).start()
    loads[5].wait()
    twin_copies[2].wait_recv()
    arrived(vbuf, v_sems.at[1])
    head_terms = [jnp.zeros((16, 224), F32)] * 2
    for yb in range(4):
        vwide[yb] = vbuf[4 * yb:4 * yb + 4].astype(F32).reshape(128, 128)
        for h in range(0, 8, 2):
            rows = jnp.concatenate(
                [vwide[yb, pl.ds(h, 16, stride=8), :], vwide[yb, pl.ds(h + 1, 16, stride=8), :]], axis=1
            ).astype(BF16)
            head = 8 * yb + h
            for e in range(2):
                head_terms[e] = head_terms[e] + nt(rows, wo[e, :, 128 * head:128 * head + 256])

    for e in range(2):
        for k in range(4):
            term = head_terms[e][4 * k:4 * k + 4]
            right = jnp.concatenate([term[:, 128:224], jnp.zeros((4, 32), F32)], axis=1)
            terms[2 * k + e] = jnp.concatenate([term[:, 0:128], right], axis=0)
    t_slot = 4 * c + x
    for to_x, to_c, device in across:
        remote(terms.at[2 * to_x + to_c], tbuf.at[t_slot], t_sems.at[0], t_sems.at[1], device).start()
    pltpu.make_async_copy(terms.at[slot], tbuf.at[t_slot], t_sems.at[1]).start()
    arrived(tbuf, t_sems.at[1])
    for e in range(2):
        result = tbuf[4 * e] + tbuf[4 * e + 1] + tbuf[4 * e + 2] + tbuf[4 * e + 3]
        result = jnp.concatenate([result[0:4], result[4:8, 0:96]], axis=1)
        if e == 0:
            lower = result
    out[...] = jnp.concatenate([result, lower], axis=0).astype(BF16)

    for copy in rope_copies + twin_copies:
        copy.wait_send()
    arrived(ybuf.at[pl.ds(0, 7)], x_sems.at[0])
    arrived(qbuf.at[pl.ds(0, 15)], q_sems.at[0])
    arrived(obuf.at[0], rs_sems.at[0, 0])
    arrived(obuf.at[1], rs_sems.at[0, 1])
    arrived(statbuf, stat_sems.at[0])
    arrived(vbuf.at[pl.ds(0, 15)], v_sems.at[0])
    arrived(tbuf.at[pl.ds(0, 7)], t_sems.at[0])


def body(q_nope, q_rope, latent_cache, rope_keys, lengths, w_uk, w_uv, w_out):
    any_spec = pl.BlockSpec(memory_space=pl.ANY)
    dma = pltpu.SemaphoreType.DMA
    return pl.pallas_call(
        kernel,
        out_shape=jax.ShapeDtypeStruct((8, 224), BF16),
        in_specs=[pl.BlockSpec(memory_space=pltpu.SMEM)] + [any_spec] * 7,
        out_specs=pl.BlockSpec(memory_space=pltpu.VMEM),
        scratch_shapes=[
            pltpu.VMEM((1024, 128), BF16),
            pltpu.VMEM((512, 128), BF16),
            pltpu.VMEM((8, 16, 128), BF16),
            pltpu.VMEM((8, 16, 128), BF16),
            pltpu.VMEM((16, 8, 16, 128), BF16),
            pltpu.VMEM((4, 128, 512), BF16),
            pltpu.VMEM((4, 4, 32, 64), BF16),
            pltpu.VMEM((4, 1024, 512), BF16),
            pltpu.VMEM((4, 64, 1024), BF16),
            pltpu.VMEM((8, 512, 128), BF16),
            pltpu.VMEM((2, 224, 4096), BF16),
            pltpu.VMEM((2, 16, 16, 512), BF16),
            pltpu.VMEM((8, 128), F32),
            pltpu.VMEM((2, 16, 16, 512), BF16),
            pltpu.VMEM((16, 8, 128), F32),
            pltpu.VMEM((128, 128), F32),
            pltpu.VMEM((32, 128), BF16),
            pltpu.VMEM((16, 32, 128), BF16),
            pltpu.VMEM((4, 128, 128), F32),
            pltpu.VMEM((8, 8, 128), F32),
            pltpu.VMEM((8, 8, 128), F32),
            dma((7,)), dma((2, 3)), dma((2, 3)), dma((2,)), dma((2,)), dma((2, 2)), dma((2,)), dma((2,)), dma((2,)),
        ],
        compiler_params=pltpu.CompilerParams(
            collective_id=0, has_side_effects=True, vmem_limit_bytes=60 << 20
        ),
    )(
        lengths,
        q_nope.reshape(1024, 128),
        q_rope,
        latent_cache,
        jnp.swapaxes(rope_keys, 1, 2),
        jnp.swapaxes(w_uk, 1, 2).reshape(512, 128),
        w_uv,
        w_out.T,
    )


def solution(mesh):
    return jax.shard_map(
        body,
        mesh=mesh,
        in_specs=(
            P(None, "head", None),
            P(None, "head", None),
            P(None, "ctx", None),
            P(None, "ctx", None),
            P(),
            P("head", None, "ctx"),
            P("head", None, None),
            P("head", "ctx"),
        ),
        out_specs=P("head", "ctx"),
        check_vma=False,
    )
```

```python
import functools

import jax
import jax.numpy as jnp
from jax import lax
from jax.experimental import pallas as pl
from jax.experimental.pallas import tpu as pltpu
from jax.sharding import PartitionSpec as P

MESH = pl.DeviceIdType.MESH
F32 = jnp.float32
BF16 = jnp.bfloat16


def nt(a, b):
    return lax.dot_general(a, b, (((1,), (1,)), ((), ())), preferred_element_type=F32)


def nn(a, b):
    return jnp.dot(a, b, preferred_element_type=F32)


def kernel(
    lengths, q_nope, q_rope, cache, keys, w_uk, w_uv, w_out, out,
    qn, wk, ybuf, xbuf, ebuf, qbuf, rbuf, cbuf, kbuf, uv, wo,
    obuf, stat, rsbuf, statbuf, wcol, vmsg, vbuf, vwide, terms, tbuf,
    load_sem, rope_sems, pair_sems, x_sems, q_sems, rs_sems, stat_sems, v_sems, t_sems, ready,
):
    ctx = lax.axis_index("ctx")
    x = lax.axis_index("head")
    chip, c = ctx // 2, ctx % 2
    z, y = chip // 4, chip % 4
    twin = ctx + 1 - 2 * c
    scale = (128 + 64) ** (-0.5)

    def remote(src, dst, send_sem, recv_sem, device):
        return pltpu.make_async_remote_copy(
            src_ref=src, dst_ref=dst, send_sem=send_sem, recv_sem=recv_sem, device_id=device, device_id_type=MESH
        )

    def arrived(ref, sem):
        pltpu.make_async_copy(ref, ref, sem).wait()

    across = []
    for k in range(1, 8):
        to_x, to_c = (x + k // 2) % 4, (c + k) % 2
        across.append((to_x, to_c, (2 * chip + to_c, to_x)))
    steps = [(a, b) for a in range(4) for b in range(4)]
    steps.sort(key=lambda s: -(min(s[0], 4 - s[0]) + min(s[1], 4 - s[1])))
    plane = [(2 * (4 * ((z + a) % 4) + (y + b) % 4) + c, x) for a, b in steps if (a, b) != (0, 0)]
    along_y = [(2 * (4 * z + (y + b) % 4) + c, x) for b in (2, 1, 3)]
    along_z = [(2 * (4 * ((z + a) % 4) + y) + c, x) for a in (2, 1, 3)]

    loads = [
        pltpu.make_async_copy(q_nope, qn, load_sem.at[0]),
        pltpu.make_async_copy(w_uk, wk, load_sem.at[1]),
    ]
    for load in loads:
        load.start()

    barrier = pltpu.get_barrier_semaphore()
    for device in along_y + along_z:
        pl.semaphore_signal(barrier, inc=1, device_id=device, device_id_type=MESH)
    for _, _, device in across:
        pl.semaphore_signal(barrier, inc=1, device_id=device, device_id_type=MESH)

    mine, theirs = 8 * x + 4 * c, 8 * x + 4 * (1 - c)
    half = pl.ds(pl.multiple_of(c * 512, 512), 512)
    later = [
        pltpu.make_async_copy(cache.at[pl.ds(mine, 4)], cbuf.at[:, half], load_sem.at[2]),
        pltpu.make_async_copy(keys.at[pl.ds(mine, 4)], kbuf.at[:, :, half], load_sem.at[3]),
        pltpu.make_async_copy(w_uv.at[pl.ds(8 * y, 8)], uv, load_sem.at[4]),
        pltpu.make_async_copy(w_out, wo.at[c], load_sem.at[5]),
        pltpu.make_async_copy(q_rope.at[pl.ds(mine, 4)], rbuf.at[x], load_sem.at[6]),
    ]
    for load in later:
        load.start()
    loads += later

    loads[0].wait()
    loads[1].wait()
    row_head = lax.broadcasted_iota(jnp.int32, (512, 128), 0) // 16
    lane_head = lax.broadcasted_iota(jnp.int32, (512, 128), 1) % 32
    own_head = row_head == lane_head
    for t in range(8):
        every = nt(wk[...], qn[pl.ds(128 * t, 128), :])
        kept = jnp.where(own_head, every, 0.0).reshape(32, 16, 128)
        ybuf[t] = jnp.sum(kept, axis=0).astype(BF16)

    pl.semaphore_wait(barrier, 13)

    slot = 2 * x + c
    for to_x, to_c, device in across:
        remote(ybuf.at[2 * to_x + to_c], xbuf.at[slot], x_sems.at[0], x_sems.at[1], device).start()
    pltpu.make_async_copy(ybuf.at[slot], xbuf.at[slot], x_sems.at[1]).start()
    for device in along_y:
        pl.semaphore_signal(ready, inc=1, device_id=device, device_id_type=MESH)
    rope_copies = []
    for k in range(1, 4):
        to = (x + k) % 4
        copy = remote(
            q_rope.at[pl.ds(8 * to + 4 * c, 4)], rbuf.at[x], rope_sems.at[0, k - 1], rope_sems.at[1, k - 1], (ctx, to)
        )
        copy.start()
        rope_copies.append(copy)
    twin_copies = [
        remote(cache.at[pl.ds(theirs, 4)], cbuf.at[:, half], pair_sems.at[0, 0], pair_sems.at[1, 0], (twin, x)),
        remote(keys.at[pl.ds(theirs, 4)], kbuf.at[:, :, half], pair_sems.at[0, 1], pair_sems.at[1, 1], (twin, x)),
        remote(w_out, wo.at[c], pair_sems.at[0, 2], pair_sems.at[1, 2], (twin, x)),
    ]
    twin_copies[0].start()
    twin_copies[1].start()

    arrived(xbuf, x_sems.at[1])
    for i in range(4):
        for e in range(2):
            ebuf[i // 2, i % 2, e] = jnp.concatenate(
                [xbuf[2 * g + e, :, 32 * i:32 * i + 32] for g in range(4)], axis=1
            )
    pl.semaphore_wait(ready, 3)
    for pair in range(2):
        for device in plane:
            remote(ebuf.at[pair], qbuf.at[pair, chip], q_sems.at[0, pair], q_sems.at[1, pair], device).start()
        pltpu.make_async_copy(ebuf.at[pair], qbuf.at[pair, chip], q_sems.at[1, pair]).start()
    twin_copies[2].start()

    loads[2].wait()
    loads[3].wait()
    loads[6].wait()
    twin_copies[0].wait_recv()
    twin_copies[1].wait_recv()
    for copy in rope_copies:
        copy.wait_recv()

    place = chip * 1024 + lax.broadcasted_iota(jnp.int32, (128, 1024), 1)
    lane = lax.broadcasted_iota(jnp.int32, (128, 128), 1)
    stats = jnp.zeros((128, 128), F32)
    owners = []
    for a, b in steps:
        to_x, to_y = (x + a) % 4, (y + b) % 4
        owners.append((4 * to_x + to_y, (2 * (4 * ((x + to_x) % 4) + to_y) + 1 - c, to_x)))
    for pair in range(2):
        weighted = []
        arrived(qbuf.at[pair], q_sems.at[1, pair])
        for i in (2 * pair, 2 * pair + 1):
            rope = rbuf[:, i].reshape(128, 64)
            query = qbuf[pair, :, i % 2].reshape(512, 128).T
            scores = (nt(query, cbuf[i]) + nn(rope, kbuf[i])) * scale
            inside = place < lengths[mine + i]
            scores = jnp.where(inside, scores, -1e30)
            peak = jnp.max(scores, axis=1, keepdims=True)
            weights = jnp.where(inside, jnp.exp(scores - peak), 0.0).astype(BF16)
            total = jnp.sum(weights.astype(F32), axis=1, keepdims=True)
            weighted.append(weights)
            stats = jnp.where(lane == i, peak, jnp.where(lane == 4 + i, total, stats))
        if pair == 1:
            stat[...] = stats.T[0:8, :]
            for _, device in owners:
                remote(stat, statbuf.at[chip], stat_sems.at[0], stat_sems.at[1], device).start()
        parts = [nn(weighted[i], cbuf[2 * pair + i]) for i in range(2)]
        for b in range(16):
            obuf[pair, b] = jnp.concatenate(
                [parts[0][8 * b:8 * b + 8], parts[1][8 * b:8 * b + 8]], axis=0
            ).astype(BF16)
        for b, device in owners:
            remote(obuf.at[pair, b], rsbuf.at[pair, chip], rs_sems.at[0, pair], rs_sems.at[1, pair], device).start()

    arrived(statbuf, stat_sems.at[1])
    peaks, totals = statbuf[:, 0:4, :], statbuf[:, 4:8, :]
    factors = jnp.exp(peaks - jnp.max(peaks, axis=0, keepdims=True))
    factors = factors / jnp.sum(factors * totals, axis=0, keepdims=True)
    factors = jnp.concatenate([factors.reshape(64, 128), jnp.zeros((64, 128), F32)], axis=0)
    wcol[...] = factors.T
    own_factors = wcol[pl.ds(pl.multiple_of(8 * (4 * x + y), 8), 8), :]
    summed = []
    for pair in range(2):
        arrived(rsbuf.at[pair], rs_sems.at[1, pair])
        acc = [jnp.zeros((8, 512), F32), jnp.zeros((8, 512), F32)]
        for d in range(16):
            chunk = rsbuf[pair, d].astype(F32)
            for i in range(2):
                at = 4 * d + 2 * pair + i
                acc[i] = acc[i] + own_factors[:, at:at + 1] * chunk[8 * i:8 * i + 8]
        summed += acc
    summed = jnp.concatenate(summed, axis=0)
    high = summed.astype(BF16)
    low = (summed - high.astype(F32)).astype(BF16)
    both = jnp.concatenate([high, low], axis=0)
    loads[4].wait()
    own_row = lax.broadcasted_iota(jnp.int32, (32, 128), 0) % 8
    values = jnp.zeros((32, 128), F32)
    for h in range(8):
        product = nn(both, uv[h])
        values = jnp.where(own_row == h, product[0:32] + product[32:64], values)
    vmsg[...] = values.astype(BF16)

    v_slot = 4 * y + (z + 4 - x) % 4
    for device in plane:
        remote(vmsg, vbuf.at[v_slot], v_sems.at[0], v_sems.at[1], device).start()
    pltpu.make_async_copy(vmsg, vbuf.at[v_slot], v_sems.at[1]).start()
    loads[5].wait()
    twin_copies[2].wait_recv()
    arrived(vbuf, v_sems.at[1])
    head_terms = [jnp.zeros((16, 224), F32)] * 2
    for yb in range(4):
        vwide[yb] = vbuf[4 * yb:4 * yb + 4].astype(F32).reshape(128, 128)
        for h in range(0, 8, 2):
            rows = jnp.concatenate(
                [vwide[yb, pl.ds(h, 16, stride=8), :], vwide[yb, pl.ds(h + 1, 16, stride=8), :]], axis=1
            ).astype(BF16)
            head = 8 * yb + h
            for e in range(2):
                head_terms[e] = head_terms[e] + nt(rows, wo[e, :, 128 * head:128 * head + 256])

    for e in range(2):
        for k in range(4):
            term = head_terms[e][4 * k:4 * k + 4]
            right = jnp.concatenate([term[:, 128:224], jnp.zeros((4, 32), F32)], axis=1)
            terms[2 * k + e] = jnp.concatenate([term[:, 0:128], right], axis=0)
    t_slot = 4 * c + x
    for to_x, to_c, device in across:
        remote(terms.at[2 * to_x + to_c], tbuf.at[t_slot], t_sems.at[0], t_sems.at[1], device).start()
    pltpu.make_async_copy(terms.at[slot], tbuf.at[t_slot], t_sems.at[1]).start()
    arrived(tbuf, t_sems.at[1])
    for e in range(2):
        result = tbuf[4 * e] + tbuf[4 * e + 1] + tbuf[4 * e + 2] + tbuf[4 * e + 3]
        result = jnp.concatenate([result[0:4], result[4:8, 0:96]], axis=1)
        if e == 0:
            lower = result
    out[...] = jnp.concatenate([result, lower], axis=0).astype(BF16)

    for copy in rope_copies + twin_copies:
        copy.wait_send()
    arrived(ybuf.at[pl.ds(0, 7)], x_sems.at[0])
    for pair in range(2):
        arrived(qbuf.at[pair, pl.ds(0, 15)], q_sems.at[0, pair])
    arrived(obuf.at[0], rs_sems.at[0, 0])
    arrived(obuf.at[1], rs_sems.at[0, 1])
    arrived(statbuf, stat_sems.at[0])
    arrived(vbuf.at[pl.ds(0, 15)], v_sems.at[0])
    arrived(tbuf.at[pl.ds(0, 7)], t_sems.at[0])


def body(q_nope, q_rope, latent_cache, rope_keys, lengths, w_uk, w_uv, w_out):
    any_spec = pl.BlockSpec(memory_space=pl.ANY)
    dma = pltpu.SemaphoreType.DMA
    return pl.pallas_call(
        kernel,
        out_shape=jax.ShapeDtypeStruct((8, 224), BF16),
        in_specs=[pl.BlockSpec(memory_space=pltpu.SMEM)] + [any_spec] * 7,
        out_specs=pl.BlockSpec(memory_space=pltpu.VMEM),
        scratch_shapes=[
            pltpu.VMEM((1024, 128), BF16),
            pltpu.VMEM((512, 128), BF16),
            pltpu.VMEM((8, 16, 128), BF16),
            pltpu.VMEM((8, 16, 128), BF16),
            pltpu.VMEM((2, 2, 2, 16, 128), BF16),
            pltpu.VMEM((2, 16, 2, 2, 16, 128), BF16),
            pltpu.VMEM((4, 4, 32, 64), BF16),
            pltpu.VMEM((4, 1024, 512), BF16),
            pltpu.VMEM((4, 64, 1024), BF16),
            pltpu.VMEM((8, 512, 128), BF16),
            pltpu.VMEM((2, 224, 4096), BF16),
            pltpu.VMEM((2, 16, 16, 512), BF16),
            pltpu.VMEM((8, 128), F32),
            pltpu.VMEM((2, 16, 16, 512), BF16),
            pltpu.VMEM((16, 8, 128), F32),
            pltpu.VMEM((128, 128), F32),
            pltpu.VMEM((32, 128), BF16),
            pltpu.VMEM((16, 32, 128), BF16),
            pltpu.VMEM((4, 128, 128), F32),
            pltpu.VMEM((8, 8, 128), F32),
            pltpu.VMEM((8, 8, 128), F32),
            dma((7,)), dma((2, 3)), dma((2, 3)), dma((2,)), dma((2, 2)), dma((2, 2)), dma((2,)), dma((2,)), dma((2,)),
            pltpu.SemaphoreType.REGULAR,
        ],
        compiler_params=pltpu.CompilerParams(
            collective_id=0, has_side_effects=True, vmem_limit_bytes=60 << 20
        ),
    )(
        lengths,
        q_nope.reshape(1024, 128),
        q_rope,
        latent_cache,
        jnp.swapaxes(rope_keys, 1, 2),
        jnp.swapaxes(w_uk, 1, 2).reshape(512, 128),
        w_uv,
        w_out.T,
    )


def solution(mesh):
    return jax.shard_map(
        body,
        mesh=mesh,
        in_specs=(
            P(None, "head", None),
            P(None, "head", None),
            P(None, "ctx", None),
            P(None, "ctx", None),
            P(),
            P("head", None, "ctx"),
            P("head", None, None),
            P("head", "ctx"),
        ),
        out_specs=P("head", "ctx"),
        check_vma=False,
    )
```

```python
import functools

import jax
import jax.numpy as jnp
from jax import lax
from jax.experimental import pallas as pl
from jax.experimental.pallas import tpu as pltpu
from jax.sharding import PartitionSpec as P

MESH = pl.DeviceIdType.MESH
F32 = jnp.float32
BF16 = jnp.bfloat16


def nt(a, b):
    return lax.dot_general(a, b, (((1,), (1,)), ((), ())), preferred_element_type=F32)


def nn(a, b):
    return jnp.dot(a, b, preferred_element_type=F32)


def kernel(
    lengths_in, q_nope, q_rope, cache, keys, w_uk, w_uv, w_out, out,
    qn, wk, ybuf, xbuf, ebuf, qbuf, rbuf, base, cbuf, kbuf, uv, wo,
    obuf, stat, rsbuf, statbuf, wcol, vmsg, vbuf, vwide, terms, tbuf,
    load_sem, rope_sems, pair_sems, x_sems, q_sems, rs_sems, stat_sems, v_sems, t_sems, uv_sems, ready, lengths,
):
    ctx = lax.axis_index("ctx")
    x = lax.axis_index("head")
    chip, c = ctx // 2, ctx % 2
    z, y = chip // 4, chip % 4
    twin = ctx + 1 - 2 * c
    scale = (128 + 64) ** (-0.5)
    group = (x + z) % 4

    def remote(src, dst, send_sem, recv_sem, device):
        return pltpu.make_async_remote_copy(
            src_ref=src, dst_ref=dst, send_sem=send_sem, recv_sem=recv_sem, device_id=device, device_id_type=MESH
        )

    def arrived(ref, sem):
        pltpu.make_async_copy(ref, ref, sem).wait()

    across = []
    for k in range(1, 8):
        to_x, to_c = (x + k // 2) % 4, (c + k) % 2
        across.append((to_x, to_c, (2 * chip + to_c, to_x)))
    steps = [(a, b) for a in range(4) for b in range(4)]
    steps.sort(key=lambda s: -(min(s[0], 4 - s[0]) + min(s[1], 4 - s[1])))
    plane = [(2 * (4 * ((z + a) % 4) + (y + b) % 4) + c, x) for a, b in steps if (a, b) != (0, 0)]
    along_y = [(2 * (4 * z + (y + b) % 4) + c, x) for b in (2, 1, 3)]
    along_z = [(2 * (4 * ((z + a) % 4) + y) + c, x) for a in (2, 1, 3)]

    loads = [
        pltpu.make_async_copy(q_nope, qn, load_sem.at[0]),
        pltpu.make_async_copy(w_uk, wk, load_sem.at[1]),
    ]
    for load in loads:
        load.start()

    barrier = pltpu.get_barrier_semaphore()
    for device in along_y + along_z:
        pl.semaphore_signal(barrier, inc=1, device_id=device, device_id_type=MESH)
    for _, _, device in across:
        pl.semaphore_signal(barrier, inc=1, device_id=device, device_id_type=MESH)

    mine, theirs = 8 * x + 4 * c, 8 * x + 4 * (1 - c)
    half = pl.ds(pl.multiple_of(c * 512, 512), 512)
    later = [
        pltpu.make_async_copy(cache.at[pl.ds(mine, 4)], cbuf.at[:, half], load_sem.at[2]),
        pltpu.make_async_copy(keys.at[pl.ds(mine, 4)], kbuf.at[:, :, half], load_sem.at[3]),
        pltpu.make_async_copy(w_out, wo.at[c], load_sem.at[5]),
        pltpu.make_async_copy(q_rope.at[pl.ds(mine, 4)], rbuf.at[x], load_sem.at[6]),
        pltpu.make_async_copy(lengths_in, lengths, load_sem.at[7]),
    ]
    for load in later:
        load.start()
    load_cache, load_keys, load_out, load_rope, load_lengths = later

    loads[0].wait()
    loads[1].wait()
    row_head = lax.broadcasted_iota(jnp.int32, (512, 128), 0) // 16
    lane_head = lax.broadcasted_iota(jnp.int32, (512, 128), 1) % 32
    own_head = row_head == lane_head
    for t in range(8):
        every = nt(wk[...], qn[pl.ds(128 * t, 128), :])
        kept = jnp.where(own_head, every, 0.0).reshape(32, 16, 128)
        ybuf[t] = jnp.sum(kept, axis=0).astype(BF16)

    pl.semaphore_wait(barrier, 13)

    slot = 2 * x + c
    for to_x, to_c, device in across:
        remote(ybuf.at[2 * to_x + to_c], xbuf.at[slot], x_sems.at[0], x_sems.at[1], device).start()
    pltpu.make_async_copy(ybuf.at[slot], xbuf.at[slot], x_sems.at[1]).start()
    for device in along_y:
        pl.semaphore_signal(ready, inc=1, device_id=device, device_id_type=MESH)
    rope_copies = []
    for k in range(1, 4):
        to = (x + k) % 4
        copy = remote(
            q_rope.at[pl.ds(8 * to + 4 * c, 4)], rbuf.at[x], rope_sems.at[0, k - 1], rope_sems.at[1, k - 1], (ctx, to)
        )
        copy.start()
        rope_copies.append(copy)
    twin_copies = [
        remote(cache.at[pl.ds(theirs, 4)], cbuf.at[:, half], pair_sems.at[0, 0], pair_sems.at[1, 0], (twin, x)),
        remote(keys.at[pl.ds(theirs, 4)], kbuf.at[:, :, half], pair_sems.at[0, 1], pair_sems.at[1, 1], (twin, x)),
        remote(w_out, wo.at[c], pair_sems.at[0, 2], pair_sems.at[1, 2], (twin, x)),
    ]
    twin_copies[0].start()
    twin_copies[1].start()
    heads = w_uv.at[pl.ds(8 * y + 4 * c, 4)]
    uv_local = pltpu.make_async_copy(heads, uv.at[c], uv_sems.at[1])
    uv_push = remote(heads, uv.at[c], uv_sems.at[0], uv_sems.at[1], (ctx, (x + 4 - z) % 4))
    pl.when(z == 0)(uv_local.start)
    pl.when(z != 0)(uv_push.start)
    uv_twin = remote(uv.at[c], uv.at[c], uv_sems.at[2], uv_sems.at[3], (twin, x))

    arrived(xbuf, x_sems.at[1])
    for i in range(4):
        for e in range(2):
            ebuf[i, e] = jnp.concatenate([xbuf[2 * g + e, :, 32 * i:32 * i + 32] for g in range(4)], axis=1)
    pl.semaphore_wait(ready, 3)
    for i in range(4):
        for device in plane:
            remote(ebuf.at[i], qbuf.at[i, chip], q_sems.at[0, i], q_sems.at[1, i], device).start()
        pltpu.make_async_copy(ebuf.at[i], qbuf.at[i, chip], q_sems.at[1, i]).start()
    twin_copies[2].start()

    load_keys.wait()
    load_rope.wait()
    load_lengths.wait()
    twin_copies[1].wait_recv()
    for copy in rope_copies:
        copy.wait_recv()
    place = chip * 1024 + lax.broadcasted_iota(jnp.int32, (128, 1024), 1)
    for i in range(4):
        base[i] = jnp.where(place < lengths[mine + i], nn(rbuf[:, i].reshape(128, 64), kbuf[i]), -1e30)
    load_cache.wait()
    twin_copies[0].wait_recv()

    def scores_of(i):
        arrived(qbuf.at[i], q_sems.at[1, i])
        return nt(qbuf[i].reshape(512, 128).T, cbuf[i]) + base[i]

    lane = lax.broadcasted_iota(jnp.int32, (128, 128), 1)
    stats = jnp.zeros((128, 128), F32)
    scores = scores_of(0)
    for i in range(4):
        peak = jnp.maximum(jnp.max(scores, axis=1, keepdims=True), -1e29)
        weights = jnp.exp2((scores - peak) * (scale * 1.4426950408889634))
        total = jnp.sum(weights, axis=1, keepdims=True)
        stats = jnp.where(lane == i, peak, jnp.where(lane == 4 + i, total, stats))
        if i < 3:
            scores = scores_of(i + 1)
        else:
            stat[...] = stats.T[0:8, :]
            for device in plane:
                remote(stat, statbuf.at[chip], stat_sems.at[0], stat_sems.at[1], device).start()
            pltpu.make_async_copy(stat, statbuf.at[chip], stat_sems.at[1]).start()
        part = nn(weights.astype(BF16), cbuf[i]).reshape(16, 8, 512)
        obuf[i] = jnp.concatenate([part[:, :, 0:256], part[:, :, 256:512]], axis=1).astype(BF16)
        for a, b in steps:
            to_z, to_y = (z + a) % 4, (y + b) % 4
            source = obuf.at[i, 4 * ((x + to_z) % 4) + to_y]
            if (a, b) == (0, 0):
                pltpu.make_async_copy(source, rsbuf.at[i, chip], rs_sems.at[1, i]).start()
            else:
                device = (2 * (4 * to_z + to_y) + c, x)
                remote(source, rsbuf.at[i, chip], rs_sems.at[0, i], rs_sems.at[1, i], device).start()
    uv_local.wait()
    uv_twin.start()

    arrived(statbuf, stat_sems.at[1])
    peaks, totals = statbuf[:, 0:4, :], statbuf[:, 4:8, :]
    factors = jnp.exp2((peaks - jnp.max(peaks, axis=0, keepdims=True)) * (scale * 1.4426950408889634))
    factors = factors / jnp.sum(factors * totals, axis=0, keepdims=True)
    factors = jnp.concatenate([factors.reshape(64, 128), jnp.zeros((64, 128), F32)], axis=0)
    wcol[...] = factors.T
    own_factors = wcol[pl.ds(pl.multiple_of(32 * group + 8 * y, 8), 8), :]
    own_factors = jnp.concatenate([own_factors, own_factors], axis=0)
    summed = []
    for i in range(4):
        arrived(rsbuf.at[i], rs_sems.at[1, i])
        acc = jnp.zeros((16, 256), F32)
        for d in range(16):
            acc = acc + own_factors[:, 4 * d + i:4 * d + i + 1] * rsbuf[i, d].astype(F32)
        summed.append(jnp.concatenate([acc[0:8], acc[8:16]], axis=1))
    summed = jnp.concatenate(summed, axis=0)
    high = summed.astype(BF16)
    low = (summed - high.astype(F32)).astype(BF16)
    both = jnp.concatenate([high, low], axis=0)
    uv_twin.wait_recv()
    own_row = lax.broadcasted_iota(jnp.int32, (32, 128), 0) % 8
    values = jnp.zeros((32, 128), F32)
    for h in range(0, 8, 2):
        product = nn(both, jnp.concatenate([uv[h // 4, h % 4], uv[h // 4, h % 4 + 1]], axis=1))
        product = product[0:32] + product[32:64]
        values = jnp.where(own_row == h, product[:, 0:128], jnp.where(own_row == h + 1, product[:, 128:256], values))
    vmsg[...] = values.astype(BF16)

    for a, b in steps:
        device = (2 * (4 * ((z + a) % 4) + (y + b) % 4) + 1 - c, group)
        remote(vmsg, vbuf.at[4 * y + x], v_sems.at[0], v_sems.at[1], device).start()
    load_out.wait()
    twin_copies[2].wait_recv()
    arrived(vbuf, v_sems.at[1])
    head_terms = [jnp.zeros((16, 224), F32)] * 2
    for k in range(4):
        vwide[k] = vbuf[4 * k:4 * k + 4].astype(F32).reshape(128, 128)
        for h in range(0, 8, 2):
            rows = jnp.concatenate(
                [vwide[k, pl.ds(h, 16, stride=8), :], vwide[k, pl.ds(h + 1, 16, stride=8), :]], axis=1
            ).astype(BF16)
            head = 8 * k + h
            for e in range(2):
                head_terms[e] = head_terms[e] + nt(rows, wo[e, :, 128 * head:128 * head + 256])

    for e in range(2):
        for k in range(4):
            term = head_terms[e][4 * k:4 * k + 4]
            right = jnp.concatenate([term[:, 128:224], jnp.zeros((4, 32), F32)], axis=1)
            terms[2 * k + e] = jnp.concatenate([term[:, 0:128], right], axis=0)
    t_slot = 4 * c + x
    for to_x, to_c, device in across:
        remote(terms.at[2 * to_x + to_c], tbuf.at[t_slot], t_sems.at[0], t_sems.at[1], device).start()
    pltpu.make_async_copy(terms.at[slot], tbuf.at[t_slot], t_sems.at[1]).start()
    arrived(tbuf, t_sems.at[1])
    for e in range(2):
        result = tbuf[4 * e] + tbuf[4 * e + 1] + tbuf[4 * e + 2] + tbuf[4 * e + 3]
        result = jnp.concatenate([result[0:4], result[4:8, 0:96]], axis=1)
        if e == 0:
            lower = result
    out[...] = jnp.concatenate([result, lower], axis=0).astype(BF16)

    for copy in rope_copies + twin_copies + [uv_twin]:
        copy.wait_send()
    pl.when(z != 0)(uv_push.wait_send)
    arrived(ybuf.at[pl.ds(0, 7)], x_sems.at[0])
    for i in range(4):
        arrived(qbuf.at[i, pl.ds(0, 15)], q_sems.at[0, i])
        arrived(rsbuf.at[i, pl.ds(0, 15)], rs_sems.at[0, i])
    arrived(statbuf.at[pl.ds(0, 15)], stat_sems.at[0])
    arrived(vbuf, v_sems.at[0])
    arrived(tbuf.at[pl.ds(0, 7)], t_sems.at[0])


def body(q_nope, q_rope, latent_cache, rope_keys, lengths, w_uk, w_uv, w_out):
    any_spec = pl.BlockSpec(memory_space=pl.ANY)
    dma = pltpu.SemaphoreType.DMA
    return pl.pallas_call(
        kernel,
        out_shape=jax.ShapeDtypeStruct((8, 224), BF16),
        in_specs=[any_spec] * 8,
        out_specs=pl.BlockSpec(memory_space=pltpu.VMEM),
        scratch_shapes=[
            pltpu.VMEM((1024, 128), BF16),
            pltpu.VMEM((512, 128), BF16),
            pltpu.VMEM((8, 16, 128), BF16),
            pltpu.VMEM((8, 16, 128), BF16),
            pltpu.VMEM((4, 2, 16, 128), BF16),
            pltpu.VMEM((4, 16, 2, 16, 128), BF16),
            pltpu.VMEM((4, 4, 32, 64), BF16),
            pltpu.VMEM((4, 128, 1024), F32),
            pltpu.VMEM((4, 1024, 512), BF16),
            pltpu.VMEM((4, 64, 1024), BF16),
            pltpu.VMEM((2, 4, 512, 128), BF16),
            pltpu.VMEM((2, 224, 4096), BF16),
            pltpu.VMEM((4, 16, 16, 256), BF16),
            pltpu.VMEM((8, 128), F32),
            pltpu.VMEM((4, 16, 16, 256), BF16),
            pltpu.VMEM((16, 8, 128), F32),
            pltpu.VMEM((128, 128), F32),
            pltpu.VMEM((32, 128), BF16),
            pltpu.VMEM((16, 32, 128), BF16),
            pltpu.VMEM((4, 128, 128), F32),
            pltpu.VMEM((8, 8, 128), F32),
            pltpu.VMEM((8, 8, 128), F32),
            dma((8,)), dma((2, 3)), dma((2, 3)), dma((2,)), dma((2, 4)), dma((2, 4)), dma((2,)), dma((2,)), dma((2,)), dma((4,)),
            pltpu.SemaphoreType.REGULAR,
            pltpu.SMEM((32,), jnp.int32),
        ],
        compiler_params=pltpu.CompilerParams(
            collective_id=0, has_side_effects=True, vmem_limit_bytes=60 << 20
        ),
    )(
        lengths,
        q_nope.reshape(1024, 128),
        q_rope,
        latent_cache,
        jnp.swapaxes(rope_keys, 1, 2),
        jnp.swapaxes(w_uk, 1, 2).reshape(512, 128),
        w_uv,
        w_out.T,
    )


def solution(mesh):
    return jax.shard_map(
        body,
        mesh=mesh,
        in_specs=(
            P(None, "head", None),
            P(None, "head", None),
            P(None, "ctx", None),
            P(None, "ctx", None),
            P(),
            P("head", None, "ctx"),
            P("head", None, None),
            P("head", "ctx"),
        ),
        out_specs=P("head", "ctx"),
        check_vma=False,
    )
```

```python
import functools

import jax
import jax.numpy as jnp
from jax import lax
from jax.experimental import pallas as pl
from jax.experimental.pallas import tpu as pltpu
from jax.sharding import PartitionSpec as P

MESH = pl.DeviceIdType.MESH
F32 = jnp.float32
BF16 = jnp.bfloat16


def nt(a, b):
    return lax.dot_general(a, b, (((1,), (1,)), ((), ())), preferred_element_type=F32)


def nn(a, b):
    return jnp.dot(a, b, preferred_element_type=F32)


def kernel(
    lengths_in, q_nope, q_rope, cache, keys, w_uk, w_uv, w_out, out,
    qn, wk, ybuf, xbuf, ebuf, qbuf, rbuf, base, cbuf, kbuf, uv, wo,
    ctbuf, wot, obuf, stat, rsbuf, statbuf, wcol, vmsg, vbuf, vwide, terms,
    load_sem, rope_sems, pair_sems, x_sems, q_sems, rs_sems, stat_sems, v_sems, t_sems, uv_sems, ready, lengths,
):
    ctx = lax.axis_index("ctx")
    x = lax.axis_index("head")
    chip, c = ctx // 2, ctx % 2
    z, y = chip // 4, chip % 4
    twin = ctx + 1 - 2 * c
    scale = (128 + 64) ** (-0.5)
    group = (x + z) % 4

    def remote(src, dst, send_sem, recv_sem, device):
        return pltpu.make_async_remote_copy(
            src_ref=src, dst_ref=dst, send_sem=send_sem, recv_sem=recv_sem, device_id=device, device_id_type=MESH
        )

    def arrived(ref, sem):
        pltpu.make_async_copy(ref, ref, sem).wait()

    across = []
    for k in range(1, 8):
        to_x, to_c = (x + k // 2) % 4, (c + k) % 2
        across.append((to_x, to_c, (2 * chip + to_c, to_x)))
    steps = [(a, b) for a in range(4) for b in range(4)]
    steps.sort(key=lambda s: -(min(s[0], 4 - s[0]) + min(s[1], 4 - s[1])))
    plane = [(2 * (4 * ((z + a) % 4) + (y + b) % 4) + c, x) for a, b in steps if (a, b) != (0, 0)]
    along_y = [(2 * (4 * z + (y + b) % 4) + c, x) for b in (2, 1, 3)]
    along_z = [(2 * (4 * ((z + a) % 4) + y) + c, x) for a in (2, 1, 3)]

    loads = [
        pltpu.make_async_copy(q_nope, qn, load_sem.at[0]),
        pltpu.make_async_copy(w_uk, wk, load_sem.at[1]),
    ]
    for load in loads:
        load.start()

    barrier = pltpu.get_barrier_semaphore()
    for device in along_y + along_z:
        pl.semaphore_signal(barrier, inc=1, device_id=device, device_id_type=MESH)
    for _, _, device in across:
        pl.semaphore_signal(barrier, inc=1, device_id=device, device_id_type=MESH)

    mine, theirs = 8 * x + 4 * c, 8 * x + 4 * (1 - c)
    half = pl.ds(pl.multiple_of(c * 512, 512), 512)
    twin_half = pl.ds(pl.multiple_of((1 - c) * 512, 512), 512)
    later = [
        pltpu.make_async_copy(cache.at[pl.ds(mine, 4)], cbuf.at[:, half], load_sem.at[2]),
        pltpu.make_async_copy(keys.at[pl.ds(mine, 4)], kbuf.at[:, :, half], load_sem.at[3]),
        pltpu.make_async_copy(w_out, wo.at[c], load_sem.at[5]),
        pltpu.make_async_copy(q_rope.at[pl.ds(mine, 4)], rbuf.at[x], load_sem.at[6]),
        pltpu.make_async_copy(lengths_in, lengths, load_sem.at[7]),
    ]
    for load in later:
        load.start()
    load_cache, load_keys, load_out, load_rope, load_lengths = later

    loads[0].wait()
    loads[1].wait()
    row_head = lax.broadcasted_iota(jnp.int32, (512, 128), 0) // 16
    lane_head = lax.broadcasted_iota(jnp.int32, (512, 128), 1) % 32
    own_head = row_head == lane_head
    for t in range(8):
        every = nt(wk[...], qn[pl.ds(128 * t, 128), :])
        kept = jnp.where(own_head, every, 0.0).reshape(32, 16, 128)
        ybuf[t] = jnp.sum(kept, axis=0).astype(BF16)

    pl.semaphore_wait(barrier, 13)

    slot = 2 * x + c
    for to_x, to_c, device in across:
        remote(ybuf.at[2 * to_x + to_c], xbuf.at[slot], x_sems.at[0], x_sems.at[1], device).start()
    pltpu.make_async_copy(ybuf.at[slot], xbuf.at[slot], x_sems.at[1]).start()
    for device in along_y:
        pl.semaphore_signal(ready, inc=1, device_id=device, device_id_type=MESH)
    rope_copies = []
    for k in range(1, 4):
        to = (x + k) % 4
        copy = remote(
            q_rope.at[pl.ds(8 * to + 4 * c, 4)], rbuf.at[x], rope_sems.at[0, k - 1], rope_sems.at[1, k - 1], (ctx, to)
        )
        copy.start()
        rope_copies.append(copy)
    twin_copies = [
        remote(cache.at[pl.ds(theirs, 4)], cbuf.at[:, half], pair_sems.at[0, 0], pair_sems.at[1, 0], (twin, x)),
        remote(keys.at[pl.ds(theirs, 4)], kbuf.at[:, :, half], pair_sems.at[0, 1], pair_sems.at[1, 1], (twin, x)),
        remote(w_out, wo.at[c], pair_sems.at[0, 2], pair_sems.at[1, 2], (twin, x)),
    ]
    twin_copies[0].start()
    twin_copies[1].start()
    heads = w_uv.at[pl.ds(8 * y + 4 * c, 4)]
    uv_local = pltpu.make_async_copy(heads, uv.at[c], uv_sems.at[1])
    uv_push = remote(heads, uv.at[c], uv_sems.at[0], uv_sems.at[1], (ctx, (x + 4 - z) % 4))
    pl.when(z == 0)(uv_local.start)
    pl.when(z != 0)(uv_push.start)
    uv_twin = remote(uv.at[c], uv.at[c], uv_sems.at[2], uv_sems.at[3], (twin, x))

    arrived(xbuf, x_sems.at[1])
    for i in range(4):
        for e in range(2):
            ebuf[i, e] = jnp.concatenate([xbuf[2 * g + e, :, 32 * i:32 * i + 32] for g in range(4)], axis=1)
    pl.semaphore_wait(ready, 3)
    for i in range(4):
        for device in plane:
            remote(ebuf.at[i], qbuf.at[i, chip], q_sems.at[0, i], q_sems.at[1, i], device).start()
        pltpu.make_async_copy(ebuf.at[i], qbuf.at[i, chip], q_sems.at[1, i]).start()
    twin_copies[2].start()

    load_keys.wait()
    load_rope.wait()
    load_lengths.wait()
    twin_copies[1].wait_recv()
    for copy in rope_copies:
        copy.wait_recv()
    place = chip * 1024 + lax.broadcasted_iota(jnp.int32, (128, 1024), 1)
    for i in range(4):
        base[i] = jnp.where(place < lengths[mine + i], nn(rbuf[:, i].reshape(128, 64), kbuf[i]), -1e30)
    load_cache.wait()
    for i in range(4):
        ctbuf[i, :, half] = cbuf[i, half, :].T
    twin_copies[0].wait_recv()
    for i in range(4):
        ctbuf[i, :, twin_half] = cbuf[i, twin_half, :].T

    def scores_of(i):
        arrived(qbuf.at[i], q_sems.at[1, i])
        return nn(qbuf[i].reshape(512, 128).T, ctbuf[i]) + base[i]

    lane = lax.broadcasted_iota(jnp.int32, (128, 128), 1)
    stats = jnp.zeros((128, 128), F32)
    scores = scores_of(0)
    for i in range(4):
        peak = jnp.maximum(jnp.max(scores, axis=1, keepdims=True), -1e29)
        weights = jnp.exp2((scores - peak) * (scale * 1.4426950408889634))
        total = jnp.sum(weights, axis=1, keepdims=True)
        stats = jnp.where(lane == i, peak, jnp.where(lane == 4 + i, total, stats))
        if i < 3:
            scores = scores_of(i + 1)
        else:
            stat[...] = stats.T[0:8, :]
            for device in plane:
                remote(stat, statbuf.at[chip], stat_sems.at[0], stat_sems.at[1], device).start()
            pltpu.make_async_copy(stat, statbuf.at[chip], stat_sems.at[1]).start()
        part = nn(weights.astype(BF16), cbuf[i]).reshape(16, 8, 512)
        obuf[i] = jnp.concatenate([part[:, :, 0:256], part[:, :, 256:512]], axis=1).astype(BF16)
        for a, b in steps:
            to_z, to_y = (z + a) % 4, (y + b) % 4
            source = obuf.at[i, 4 * ((x + to_z) % 4) + to_y]
            if (a, b) == (0, 0):
                pltpu.make_async_copy(source, rsbuf.at[i, chip], rs_sems.at[1, i]).start()
            else:
                device = (2 * (4 * to_z + to_y) + c, x)
                remote(source, rsbuf.at[i, chip], rs_sems.at[0, i], rs_sems.at[1, i], device).start()
    uv_local.wait()
    uv_twin.start()
    load_out.wait()
    twin_copies[2].wait_recv()
    for e in range(2):
        for k in range(4):
            lanes = slice(1024 * k, 1024 * k + 1024)
            wot[lanes, 256 * e:256 * e + 256] = jnp.concatenate([wo[e, :, lanes], jnp.zeros((32, 1024), BF16)], axis=0).T

    arrived(statbuf, stat_sems.at[1])
    peaks, totals = statbuf[:, 0:4, :], statbuf[:, 4:8, :]
    factors = jnp.exp2((peaks - jnp.max(peaks, axis=0, keepdims=True)) * (scale * 1.4426950408889634))
    factors = factors / jnp.sum(factors * totals, axis=0, keepdims=True)
    factors = jnp.concatenate([factors.reshape(64, 128), jnp.zeros((64, 128), F32)], axis=0)
    wcol[...] = factors.T
    own_factors = wcol[pl.ds(pl.multiple_of(32 * group + 8 * y, 8), 8), :]
    own_factors = jnp.concatenate([own_factors, own_factors], axis=0)
    summed = []
    for i in range(4):
        arrived(rsbuf.at[i], rs_sems.at[1, i])
        acc = jnp.zeros((16, 256), F32)
        for d in range(16):
            acc = acc + own_factors[:, 4 * d + i:4 * d + i + 1] * rsbuf[i, d].astype(F32)
        summed.append(jnp.concatenate([acc[0:8], acc[8:16]], axis=1))
    summed = jnp.concatenate(summed, axis=0)
    high = summed.astype(BF16)
    low = (summed - high.astype(F32)).astype(BF16)
    both = jnp.concatenate([high, low], axis=0)
    uv_twin.wait_recv()
    own_row = lax.broadcasted_iota(jnp.int32, (32, 128), 0) % 8
    values = jnp.zeros((32, 128), F32)
    for h in range(0, 8, 2):
        product = nn(both, jnp.concatenate([uv[h // 4, h % 4], uv[h // 4, h % 4 + 1]], axis=1))
        product = product[0:32] + product[32:64]
        values = jnp.where(own_row == h, product[:, 0:128], jnp.where(own_row == h + 1, product[:, 128:256], values))
    vmsg[...] = values.astype(BF16)

    for a, b in steps:
        device = (2 * (4 * ((z + a) % 4) + (y + b) % 4) + 1 - c, group)
        remote(vmsg, vbuf.at[4 * y + x], v_sems.at[0], v_sems.at[1], device).start()
    arrived(vbuf, v_sems.at[1])
    head_terms = jnp.zeros((16, 512), F32)
    for k in range(4):
        vwide[k] = vbuf[4 * k:4 * k + 4].astype(F32).reshape(128, 128)
        for h in range(0, 8, 2):
            rows = jnp.concatenate(
                [vwide[k, pl.ds(h, 16, stride=8), :], vwide[k, pl.ds(h + 1, 16, stride=8), :]], axis=1
            ).astype(BF16)
            head = 8 * k + h
            head_terms = head_terms + nn(rows, wot[128 * head:128 * head + 256, :])

    rows_c = lax.broadcasted_iota(jnp.int32, (8, 256), 0) // 4 == 1 - c
    for e in range(2):
        for k in range(4):
            term = head_terms[4 * k:4 * k + 4, 256 * e:256 * e + 256]
            terms[2 * k + e] = jnp.where(rows_c, jnp.concatenate([term, term], axis=0), 0.0)
    t_slot = 4 * c + x
    for to_x, to_c, device in across:
        remote(terms.at[2 * to_x + to_c], out.at[t_slot], t_sems.at[0], t_sems.at[1], device).start()
    pltpu.make_async_copy(terms.at[slot], out.at[t_slot], t_sems.at[1]).start()
    arrived(out, t_sems.at[1])

    for copy in rope_copies + twin_copies + [uv_twin]:
        copy.wait_send()
    pl.when(z != 0)(uv_push.wait_send)
    arrived(ybuf.at[pl.ds(0, 7)], x_sems.at[0])
    for i in range(4):
        arrived(qbuf.at[i, pl.ds(0, 15)], q_sems.at[0, i])
        arrived(rsbuf.at[i, pl.ds(0, 15)], rs_sems.at[0, i])
    arrived(statbuf.at[pl.ds(0, 15)], stat_sems.at[0])
    arrived(vbuf, v_sems.at[0])
    arrived(terms.at[pl.ds(0, 7)], t_sems.at[0])


def body(q_nope, q_rope, latent_cache, rope_keys, lengths, w_uk, w_uv, w_out):
    any_spec = pl.BlockSpec(memory_space=pl.ANY)
    dma = pltpu.SemaphoreType.DMA
    terms = pl.pallas_call(
        kernel,
        out_shape=jax.ShapeDtypeStruct((8, 8, 256), F32),
        in_specs=[any_spec] * 8,
        out_specs=any_spec,
        scratch_shapes=[
            pltpu.VMEM((1024, 128), BF16),
            pltpu.VMEM((512, 128), BF16),
            pltpu.VMEM((8, 16, 128), BF16),
            pltpu.VMEM((8, 16, 128), BF16),
            pltpu.VMEM((4, 2, 16, 128), BF16),
            pltpu.VMEM((4, 16, 2, 16, 128), BF16),
            pltpu.VMEM((4, 4, 32, 64), BF16),
            pltpu.VMEM((4, 128, 1024), F32),
            pltpu.VMEM((4, 1024, 512), BF16),
            pltpu.VMEM((4, 64, 1024), BF16),
            pltpu.VMEM((2, 4, 512, 128), BF16),
            pltpu.VMEM((2, 224, 4096), BF16),
            pltpu.VMEM((4, 512, 1024), BF16),
            pltpu.VMEM((4096, 512), BF16),
            pltpu.VMEM((4, 16, 16, 256), BF16),
            pltpu.VMEM((8, 128), F32),
            pltpu.VMEM((4, 16, 16, 256), BF16),
            pltpu.VMEM((16, 8, 128), F32),
            pltpu.VMEM((128, 128), F32),
            pltpu.VMEM((32, 128), BF16),
            pltpu.VMEM((16, 32, 128), BF16),
            pltpu.VMEM((4, 128, 128), F32),
            pltpu.VMEM((8, 8, 256), F32),
            dma((8,)), dma((2, 3)), dma((2, 3)), dma((2,)), dma((2, 4)), dma((2, 4)), dma((2,)), dma((2,)), dma((2,)), dma((4,)),
            pltpu.SemaphoreType.REGULAR,
            pltpu.SMEM((32,), jnp.int32),
        ],
        compiler_params=pltpu.CompilerParams(
            collective_id=0, has_side_effects=True, vmem_limit_bytes=48 << 20
        ),
    )(
        *(
            pltpu.with_memory_space_constraint(operand, pltpu.HBM)
            for operand in (
                lengths,
                q_nope.reshape(1024, 128),
                q_rope,
                latent_cache,
                jnp.swapaxes(rope_keys, 1, 2),
                jnp.swapaxes(w_uk, 1, 2).reshape(512, 128),
                w_uv,
                w_out.T,
            )
        )
    )
    return jnp.sum(terms, axis=0)[:, 0:224].astype(BF16)


def solution(mesh):
    return jax.shard_map(
        body,
        mesh=mesh,
        in_specs=(
            P(None, "head", None),
            P(None, "head", None),
            P(None, "ctx", None),
            P(None, "ctx", None),
            P(),
            P("head", None, "ctx"),
            P("head", None, None),
            P("head", "ctx"),
        ),
        out_specs=P("head", "ctx"),
        check_vma=False,
    )
```

```python
import functools

import jax
import jax.numpy as jnp
from jax import lax
from jax.experimental import pallas as pl
from jax.experimental.pallas import tpu as pltpu
from jax.sharding import PartitionSpec as P

MESH = pl.DeviceIdType.MESH
F32 = jnp.float32
BF16 = jnp.bfloat16


def nt(a, b):
    return lax.dot_general(a, b, (((1,), (1,)), ((), ())), preferred_element_type=F32)


def nn(a, b):
    return jnp.dot(a, b, preferred_element_type=F32)


def kernel(
    lengths_in, q_nope, q_rope, cache, keys, w_uk, w_uv, w_out, out,
    qn, wk, ybuf, xbuf, ebuf, qbuf, rbuf, base, cbuf, kbuf, uv, wo,
    ctbuf, wot, obuf, stat, rsbuf, statbuf, wcol, vmsg, vbuf, vwide, terms,
    load_sem, rope_sems, pair_sems, x_sems, q_sems, rs_sems, stat_sems, v_sems, t_sems, uv_sems, ready, lengths,
):
    ctx = lax.axis_index("ctx")
    x = lax.axis_index("head")
    chip, c = ctx // 2, ctx % 2
    z, y = chip // 4, chip % 4
    twin = ctx + 1 - 2 * c
    scale = (128 + 64) ** (-0.5)
    group = (x + z) % 4

    def remote(src, dst, send_sem, recv_sem, device):
        return pltpu.make_async_remote_copy(
            src_ref=src, dst_ref=dst, send_sem=send_sem, recv_sem=recv_sem, device_id=device, device_id_type=MESH
        )

    def arrived(ref, sem):
        pltpu.make_async_copy(ref, ref, sem).wait()

    across = []
    for k in range(1, 8):
        to_x, to_c = (x + k // 2) % 4, (c + k) % 2
        across.append((to_x, to_c, (2 * chip + to_c, to_x)))
    steps = [(a, b) for a in range(4) for b in range(4)]
    steps.sort(key=lambda s: -(min(s[0], 4 - s[0]) + min(s[1], 4 - s[1])))
    plane = [(2 * (4 * ((z + a) % 4) + (y + b) % 4) + c, x) for a, b in steps if (a, b) != (0, 0)]
    along_y = [(2 * (4 * z + (y + b) % 4) + c, x) for b in (2, 1, 3)]
    along_z = [(2 * (4 * ((z + a) % 4) + y) + c, x) for a in (2, 1, 3)]

    loads = [
        pltpu.make_async_copy(q_nope, qn, load_sem.at[0]),
        pltpu.make_async_copy(w_uk, wk, load_sem.at[1]),
    ]
    for load in loads:
        load.start()

    barrier = pltpu.get_barrier_semaphore()
    for device in along_y + along_z:
        pl.semaphore_signal(barrier, inc=1, device_id=device, device_id_type=MESH)
    for _, _, device in across:
        pl.semaphore_signal(barrier, inc=1, device_id=device, device_id_type=MESH)

    mine, theirs = 8 * x + 4 * c, 8 * x + 4 * (1 - c)
    half = pl.ds(pl.multiple_of(c * 512, 512), 512)
    twin_half = pl.ds(pl.multiple_of((1 - c) * 512, 512), 512)
    later = [
        pltpu.make_async_copy(cache.at[pl.ds(mine, 4)], cbuf.at[:, half], load_sem.at[2]),
        pltpu.make_async_copy(keys.at[pl.ds(mine, 4)], kbuf.at[:, :, half], load_sem.at[3]),
        pltpu.make_async_copy(w_out, wo.at[c], load_sem.at[5]),
        pltpu.make_async_copy(q_rope.at[pl.ds(mine, 4)], rbuf.at[x], load_sem.at[6]),
        pltpu.make_async_copy(lengths_in, lengths, load_sem.at[7]),
    ]
    for load in later:
        load.start()
    load_cache, load_keys, load_out, load_rope, load_lengths = later

    loads[0].wait()
    loads[1].wait()
    row_head = lax.broadcasted_iota(jnp.int32, (512, 128), 0) // 16
    lane_head = lax.broadcasted_iota(jnp.int32, (512, 128), 1) % 32
    own_head = row_head == lane_head
    for t in range(8):
        every = nt(wk[...], qn[pl.ds(128 * t, 128), :])
        kept = jnp.where(own_head, every, 0.0).reshape(32, 16, 128)
        ybuf[t] = jnp.sum(kept, axis=0).astype(BF16)

    pl.semaphore_wait(barrier, 13)

    slot = 2 * x + c
    for to_x, to_c, device in across:
        remote(ybuf.at[2 * to_x + to_c], xbuf.at[slot], x_sems.at[0], x_sems.at[1], device).start()
    pltpu.make_async_copy(ybuf.at[slot], xbuf.at[slot], x_sems.at[1]).start()
    for device in along_y:
        pl.semaphore_signal(ready, inc=1, device_id=device, device_id_type=MESH)
    rope_copies = []
    for k in range(1, 4):
        to = (x + k) % 4
        copy = remote(
            q_rope.at[pl.ds(8 * to + 4 * c, 4)], rbuf.at[x], rope_sems.at[0, k - 1], rope_sems.at[1, k - 1], (ctx, to)
        )
        copy.start()
        rope_copies.append(copy)
    twin_copies = [
        remote(cache.at[pl.ds(theirs, 4)], cbuf.at[:, half], pair_sems.at[0, 0], pair_sems.at[1, 0], (twin, x)),
        remote(keys.at[pl.ds(theirs, 4)], kbuf.at[:, :, half], pair_sems.at[0, 1], pair_sems.at[1, 1], (twin, x)),
        remote(w_out, wo.at[c], pair_sems.at[0, 2], pair_sems.at[1, 2], (twin, x)),
    ]
    twin_copies[0].start()
    twin_copies[1].start()
    heads = w_uv.at[pl.ds(8 * y + 4 * c, 4)]
    uv_local = pltpu.make_async_copy(heads, uv.at[c], uv_sems.at[1])
    uv_push = remote(heads, uv.at[c], uv_sems.at[0], uv_sems.at[1], (ctx, (x + 4 - z) % 4))
    pl.when(z == 0)(uv_local.start)
    pl.when(z != 0)(uv_push.start)
    uv_twin = remote(uv.at[c], uv.at[c], uv_sems.at[2], uv_sems.at[3], (twin, x))

    arrived(xbuf, x_sems.at[1])
    for i in range(4):
        for e in range(2):
            ebuf[i, e] = jnp.concatenate([xbuf[2 * g + e, :, 32 * i:32 * i + 32] for g in range(4)], axis=1)
    pl.semaphore_wait(ready, 3)
    for i in range(4):
        for device in plane:
            remote(ebuf.at[i], qbuf.at[i, chip], q_sems.at[0, i], q_sems.at[1, i], device).start()
        pltpu.make_async_copy(ebuf.at[i], qbuf.at[i, chip], q_sems.at[1, i]).start()
    twin_copies[2].start()

    load_keys.wait()
    load_rope.wait()
    load_lengths.wait()
    twin_copies[1].wait_recv()
    for copy in rope_copies:
        copy.wait_recv()
    place = chip * 1024 + lax.broadcasted_iota(jnp.int32, (128, 1024), 1)
    for i in range(4):
        base[i] = jnp.where(place < lengths[mine + i], nn(rbuf[:, i].reshape(128, 64), kbuf[i]), -1e30)
    load_cache.wait()
    for i in range(4):
        ctbuf[i, :, half] = cbuf[i, half, :].T
    twin_copies[0].wait_recv()
    for i in range(4):
        ctbuf[i, :, twin_half] = cbuf[i, twin_half, :].T

    def scores_of(i):
        arrived(qbuf.at[i], q_sems.at[1, i])
        return nn(qbuf[i].reshape(512, 128).T, ctbuf[i]) + base[i]

    lane = lax.broadcasted_iota(jnp.int32, (128, 128), 1)
    stats = jnp.zeros((128, 128), F32)
    scores = scores_of(0)
    for i in range(4):
        peak = jnp.maximum(jnp.max(scores, axis=1, keepdims=True), -1e29)
        weights = jnp.exp2((scores - peak) * (scale * 1.4426950408889634))
        total = jnp.sum(weights, axis=1, keepdims=True)
        stats = jnp.where(lane == i, peak, jnp.where(lane == 4 + i, total, stats))
        if i < 3:
            scores = scores_of(i + 1)
        else:
            stat[...] = stats.T[0:8, :]
            for device in plane:
                remote(stat, statbuf.at[chip], stat_sems.at[0], stat_sems.at[1], device).start()
            pltpu.make_async_copy(stat, statbuf.at[chip], stat_sems.at[1]).start()
        part = nn(weights.astype(BF16), cbuf[i]).reshape(16, 8, 512)
        obuf[i] = jnp.concatenate([part[:, :, 0:256], part[:, :, 256:512]], axis=1).astype(BF16)
        for a, b in steps:
            to_z, to_y = (z + a) % 4, (y + b) % 4
            source = obuf.at[i, 4 * ((x + to_z) % 4) + to_y]
            if (a, b) == (0, 0):
                pltpu.make_async_copy(source, rsbuf.at[i, chip], rs_sems.at[1, i]).start()
            else:
                device = (2 * (4 * to_z + to_y) + c, x)
                remote(source, rsbuf.at[i, chip], rs_sems.at[0, i], rs_sems.at[1, i], device).start()
    uv_local.wait()
    uv_twin.start()
    load_out.wait()
    twin_copies[2].wait_recv()
    for e in range(2):
        for k in range(4):
            lanes = slice(1024 * k, 1024 * k + 1024)
            wot[k, :, 256 * e:256 * e + 256] = jnp.concatenate([wo[e, :, lanes], jnp.zeros((32, 1024), BF16)], axis=0).T

    arrived(statbuf, stat_sems.at[1])
    peaks, totals = statbuf[:, 0:4, :], statbuf[:, 4:8, :]
    factors = jnp.exp2((peaks - jnp.max(peaks, axis=0, keepdims=True)) * (scale * 1.4426950408889634))
    factors = factors / jnp.sum(factors * totals, axis=0, keepdims=True)
    factors = jnp.concatenate([factors.reshape(64, 128), jnp.zeros((64, 128), F32)], axis=0)
    wcol[...] = factors.T
    own_factors = wcol[pl.ds(pl.multiple_of(32 * group + 8 * y, 8), 8), :]
    own_factors = jnp.concatenate([own_factors, own_factors], axis=0)
    summed = []
    for i in range(4):
        arrived(rsbuf.at[i], rs_sems.at[1, i])
        acc = jnp.zeros((16, 256), F32)
        for d in range(16):
            acc = acc + own_factors[:, 4 * d + i:4 * d + i + 1] * rsbuf[i, d].astype(F32)
        summed.append(jnp.concatenate([acc[0:8], acc[8:16]], axis=1))
    summed = jnp.concatenate(summed, axis=0)
    high = summed.astype(BF16)
    low = (summed - high.astype(F32)).astype(BF16)
    both = jnp.concatenate([high, low], axis=0)
    uv_twin.wait_recv()
    own_row = lax.broadcasted_iota(jnp.int32, (32, 128), 0) % 8
    values = jnp.zeros((32, 128), F32)
    for h in range(0, 8, 2):
        product = nn(both, jnp.concatenate([uv[h // 4, h % 4], uv[h // 4, h % 4 + 1]], axis=1))
        product = product[0:32] + product[32:64]
        values = jnp.where(own_row == h, product[:, 0:128], jnp.where(own_row == h + 1, product[:, 128:256], values))
    vmsg[...] = values.astype(BF16)

    for a, b in steps:
        device = (2 * (4 * ((z + a) % 4) + (y + b) % 4) + 1 - c, group)
        remote(vmsg, vbuf.at[y, x], v_sems.at[4], v_sems.at[y], device).start()
    head_terms = jnp.zeros((16, 512), F32)
    for k in range(4):
        from_y = (y + k) % 4
        arrived(vbuf.at[from_y], v_sems.at[from_y])
        vwide[k] = vbuf[from_y].astype(F32).reshape(128, 128)
        for h in range(0, 8, 2):
            rows = jnp.concatenate(
                [vwide[k, pl.ds(h, 16, stride=8), :], vwide[k, pl.ds(h + 1, 16, stride=8), :]], axis=1
            ).astype(BF16)
            head_terms = head_terms + nn(rows, wot[from_y, 128 * h:128 * h + 256, :])

    rows_c = lax.broadcasted_iota(jnp.int32, (8, 256), 0) // 4 == 1 - c
    for e in range(2):
        for k in range(4):
            term = head_terms[4 * k:4 * k + 4, 256 * e:256 * e + 256]
            terms[2 * k + e] = jnp.where(rows_c, jnp.concatenate([term, term], axis=0), 0.0)
    t_slot = 4 * c + x
    for to_x, to_c, device in across:
        remote(terms.at[2 * to_x + to_c], out.at[t_slot], t_sems.at[0], t_sems.at[1], device).start()
    pltpu.make_async_copy(terms.at[slot], out.at[t_slot], t_sems.at[1]).start()
    arrived(out, t_sems.at[1])

    for copy in rope_copies + twin_copies + [uv_twin]:
        copy.wait_send()
    pl.when(z != 0)(uv_push.wait_send)
    arrived(ybuf.at[pl.ds(0, 7)], x_sems.at[0])
    for i in range(4):
        arrived(qbuf.at[i, pl.ds(0, 15)], q_sems.at[0, i])
        arrived(rsbuf.at[i, pl.ds(0, 15)], rs_sems.at[0, i])
    arrived(statbuf.at[pl.ds(0, 15)], stat_sems.at[0])
    arrived(vbuf, v_sems.at[4])
    arrived(terms.at[pl.ds(0, 7)], t_sems.at[0])


def body(q_nope, q_rope, latent_cache, rope_keys, lengths, w_uk, w_uv, w_out):
    any_spec = pl.BlockSpec(memory_space=pl.ANY)
    dma = pltpu.SemaphoreType.DMA
    terms = pl.pallas_call(
        kernel,
        out_shape=jax.ShapeDtypeStruct((8, 8, 256), F32),
        in_specs=[any_spec] * 8,
        out_specs=any_spec,
        scratch_shapes=[
            pltpu.VMEM((1024, 128), BF16),
            pltpu.VMEM((512, 128), BF16),
            pltpu.VMEM((8, 16, 128), BF16),
            pltpu.VMEM((8, 16, 128), BF16),
            pltpu.VMEM((4, 2, 16, 128), BF16),
            pltpu.VMEM((4, 16, 2, 16, 128), BF16),
            pltpu.VMEM((4, 4, 32, 64), BF16),
            pltpu.VMEM((4, 128, 1024), F32),
            pltpu.VMEM((4, 1024, 512), BF16),
            pltpu.VMEM((4, 64, 1024), BF16),
            pltpu.VMEM((2, 4, 512, 128), BF16),
            pltpu.VMEM((2, 224, 4096), BF16),
            pltpu.VMEM((4, 512, 1024), BF16),
            pltpu.VMEM((4, 1024, 512), BF16),
            pltpu.VMEM((4, 16, 16, 256), BF16),
            pltpu.VMEM((8, 128), F32),
            pltpu.VMEM((4, 16, 16, 256), BF16),
            pltpu.VMEM((16, 8, 128), F32),
            pltpu.VMEM((128, 128), F32),
            pltpu.VMEM((32, 128), BF16),
            pltpu.VMEM((4, 4, 32, 128), BF16),
            pltpu.VMEM((4, 128, 128), F32),
            pltpu.VMEM((8, 8, 256), F32),
            dma((8,)), dma((2, 3)), dma((2, 3)), dma((2,)), dma((2, 4)), dma((2, 4)), dma((2,)), dma((5,)), dma((2,)), dma((4,)),
            pltpu.SemaphoreType.REGULAR,
            pltpu.SMEM((32,), jnp.int32),
        ],
        compiler_params=pltpu.CompilerParams(
            collective_id=0, has_side_effects=True, vmem_limit_bytes=48 << 20
        ),
    )(
        *(
            pltpu.with_memory_space_constraint(operand, pltpu.HBM)
            for operand in (
                lengths,
                q_nope.reshape(1024, 128),
                q_rope,
                latent_cache,
                jnp.swapaxes(rope_keys, 1, 2),
                jnp.swapaxes(w_uk, 1, 2).reshape(512, 128),
                w_uv,
                w_out.T,
            )
        )
    )
    return jnp.sum(terms, axis=0)[:, 0:224].astype(BF16)


def solution(mesh):
    return jax.shard_map(
        body,
        mesh=mesh,
        in_specs=(
            P(None, "head", None),
            P(None, "head", None),
            P(None, "ctx", None),
            P(None, "ctx", None),
            P(),
            P("head", None, "ctx"),
            P("head", None, None),
            P("head", "ctx"),
        ),
        out_specs=P("head", "ctx"),
        check_vma=False,
    )
```

```python
import functools

import jax
import jax.numpy as jnp
from jax import lax
from jax.experimental import pallas as pl
from jax.experimental.pallas import tpu as pltpu
from jax.sharding import PartitionSpec as P

MESH = pl.DeviceIdType.MESH
F32 = jnp.float32
BF16 = jnp.bfloat16


def nt(a, b):
    return lax.dot_general(a, b, (((1,), (1,)), ((), ())), preferred_element_type=F32)


def nn(a, b):
    return jnp.dot(a, b, preferred_element_type=F32)


def kernel(
    lengths_in, q_nope, q_rope, cache, keys, w_uk, w_uv, w_out, out,
    qn, wk, ybuf, xbuf, ebuf, qbuf, rbuf, base, cbuf, kbuf, uv, wo,
    ctbuf, wot, obuf, stat, rsbuf, statbuf, wcol, vmsg, vbuf, vwide, terms,
    load_sem, rope_sems, pair_sems, x_sems, q_sems, rs_sems, stat_sems, v_sems, t_sems, uv_sems, ready, lengths,
):
    ctx = lax.axis_index("ctx")
    x = lax.axis_index("head")
    chip, c = ctx // 2, ctx % 2
    z, y = chip // 4, chip % 4
    twin = ctx + 1 - 2 * c
    scale = (128 + 64) ** (-0.5)
    shift = (z + 2 * c) % 4
    group = (x + shift) % 4

    def remote(src, dst, send_sem, recv_sem, device):
        return pltpu.make_async_remote_copy(
            src_ref=src, dst_ref=dst, send_sem=send_sem, recv_sem=recv_sem, device_id=device, device_id_type=MESH
        )

    def arrived(ref, sem):
        pltpu.make_async_copy(ref, ref, sem).wait()

    across = []
    for k in range(1, 8):
        to_x, to_c = (x + k // 2) % 4, (c + k) % 2
        across.append((to_x, to_c, (2 * chip + to_c, to_x)))
    steps = [(a, b) for a in range(4) for b in range(4)]
    steps.sort(key=lambda s: -(min(s[0], 4 - s[0]) + min(s[1], 4 - s[1])))
    plane = [(2 * (4 * ((z + a) % 4) + (y + b) % 4) + c, x) for a, b in steps if (a, b) != (0, 0)]
    along_y = [(2 * (4 * z + (y + b) % 4) + c, x) for b in (2, 1, 3)]
    along_z = [(2 * (4 * ((z + a) % 4) + y) + c, x) for a in (2, 1, 3)]

    loads = [
        pltpu.make_async_copy(q_nope, qn, load_sem.at[0]),
        pltpu.make_async_copy(w_uk, wk, load_sem.at[1]),
    ]
    for load in loads:
        load.start()

    barrier = pltpu.get_barrier_semaphore()
    for device in along_y + along_z:
        pl.semaphore_signal(barrier, inc=1, device_id=device, device_id_type=MESH)
    for _, _, device in across:
        pl.semaphore_signal(barrier, inc=1, device_id=device, device_id_type=MESH)

    mine, theirs = 8 * x + 4 * c, 8 * x + 4 * (1 - c)
    half = pl.ds(pl.multiple_of(c * 512, 512), 512)
    twin_half = pl.ds(pl.multiple_of((1 - c) * 512, 512), 512)
    later = [
        pltpu.make_async_copy(cache.at[pl.ds(mine, 4)], cbuf.at[:, half], load_sem.at[2]),
        pltpu.make_async_copy(keys.at[pl.ds(mine, 4)], kbuf.at[:, :, half], load_sem.at[3]),
        pltpu.make_async_copy(w_out, wo.at[c], load_sem.at[5]),
        pltpu.make_async_copy(q_rope.at[pl.ds(mine, 4)], rbuf.at[x], load_sem.at[6]),
        pltpu.make_async_copy(lengths_in, lengths, load_sem.at[7]),
    ]
    for load in later:
        load.start()
    load_cache, load_keys, load_out, load_rope, load_lengths = later

    loads[0].wait()
    loads[1].wait()
    row_head = lax.broadcasted_iota(jnp.int32, (512, 128), 0) // 16
    lane_head = lax.broadcasted_iota(jnp.int32, (512, 128), 1) % 32
    own_head = row_head == lane_head
    for t in range(8):
        every = nt(wk[...], qn[pl.ds(128 * t, 128), :])
        kept = jnp.where(own_head, every, 0.0).reshape(32, 16, 128)
        ybuf[t] = jnp.sum(kept, axis=0).astype(BF16)

    pl.semaphore_wait(barrier, 13)

    slot = 2 * x + c
    for to_x, to_c, device in across:
        remote(ybuf.at[2 * to_x + to_c], xbuf.at[slot], x_sems.at[0], x_sems.at[1], device).start()
    pltpu.make_async_copy(ybuf.at[slot], xbuf.at[slot], x_sems.at[1]).start()
    for device in along_y:
        pl.semaphore_signal(ready, inc=1, device_id=device, device_id_type=MESH)
    rope_copies = []
    for k in range(1, 4):
        to = (x + k) % 4
        copy = remote(
            q_rope.at[pl.ds(8 * to + 4 * c, 4)], rbuf.at[x], rope_sems.at[0, k - 1], rope_sems.at[1, k - 1], (ctx, to)
        )
        copy.start()
        rope_copies.append(copy)
    twin_copies = [
        remote(cache.at[pl.ds(theirs, 4)], cbuf.at[:, half], pair_sems.at[0, 0], pair_sems.at[1, 0], (twin, x)),
        remote(keys.at[pl.ds(theirs, 4)], kbuf.at[:, :, half], pair_sems.at[0, 1], pair_sems.at[1, 1], (twin, x)),
        remote(w_out, wo.at[c], pair_sems.at[0, 2], pair_sems.at[1, 2], (twin, x)),
    ]
    twin_copies[0].start()
    twin_copies[1].start()
    heads = w_uv.at[pl.ds(8 * y, 8)]
    uv_local = pltpu.make_async_copy(heads, uv, uv_sems.at[1])
    uv_push = remote(heads, uv, uv_sems.at[0], uv_sems.at[1], (ctx, (x + 4 - shift) % 4))
    pl.when(shift == 0)(uv_local.start)
    pl.when(shift != 0)(uv_push.start)

    arrived(xbuf, x_sems.at[1])
    for i in range(4):
        for e in range(2):
            ebuf[i, e] = jnp.concatenate([xbuf[2 * g + e, :, 32 * i:32 * i + 32] for g in range(4)], axis=1)
    pl.semaphore_wait(ready, 3)
    for i in range(4):
        for device in plane:
            remote(ebuf.at[i], qbuf.at[i, chip], q_sems.at[0, i], q_sems.at[1, i], device).start()
        pltpu.make_async_copy(ebuf.at[i], qbuf.at[i, chip], q_sems.at[1, i]).start()
    twin_copies[2].start()

    load_keys.wait()
    load_rope.wait()
    load_lengths.wait()
    twin_copies[1].wait_recv()
    for copy in rope_copies:
        copy.wait_recv()
    place = chip * 1024 + lax.broadcasted_iota(jnp.int32, (128, 1024), 1)
    for i in range(4):
        base[i] = jnp.where(place < lengths[mine + i], nn(rbuf[:, i].reshape(128, 64), kbuf[i]), -1e30)
    load_cache.wait()
    for i in range(4):
        ctbuf[i, :, half] = cbuf[i, half, :].T
    twin_copies[0].wait_recv()
    for i in range(4):
        ctbuf[i, :, twin_half] = cbuf[i, twin_half, :].T

    def scores_of(i):
        arrived(qbuf.at[i], q_sems.at[1, i])
        return nn(qbuf[i].reshape(512, 128).T, ctbuf[i]) + base[i]

    lane = lax.broadcasted_iota(jnp.int32, (128, 128), 1)
    stats = jnp.zeros((128, 128), F32)
    scores = scores_of(0)
    for i in range(4):
        peak = jnp.maximum(jnp.max(scores, axis=1, keepdims=True), -1e29)
        weights = jnp.exp2((scores - peak) * (scale * 1.4426950408889634))
        total = jnp.sum(weights, axis=1, keepdims=True)
        stats = jnp.where(lane == i, peak, jnp.where(lane == 4 + i, total, stats))
        if i < 3:
            scores = scores_of(i + 1)
        else:
            stat[...] = stats.T[0:8, :]
            for device in plane:
                remote(stat, statbuf.at[chip], stat_sems.at[0], stat_sems.at[1], device).start()
            pltpu.make_async_copy(stat, statbuf.at[chip], stat_sems.at[1]).start()
        part = nn(weights.astype(BF16), cbuf[i]).reshape(16, 8, 512)
        obuf[i] = jnp.concatenate([part[:, :, 0:256], part[:, :, 256:512]], axis=1).astype(BF16)
        for a, b in steps:
            to_z, to_y = (z + a) % 4, (y + b) % 4
            source = obuf.at[i, 4 * ((x + to_z + 2 * c) % 4) + to_y]
            if (a, b) == (0, 0):
                pltpu.make_async_copy(source, rsbuf.at[i, chip], rs_sems.at[1, i]).start()
            else:
                device = (2 * (4 * to_z + to_y) + c, x)
                remote(source, rsbuf.at[i, chip], rs_sems.at[0, i], rs_sems.at[1, i], device).start()
    load_out.wait()
    twin_copies[2].wait_recv()
    for e in range(2):
        for k in range(4):
            lanes = slice(1024 * k, 1024 * k + 1024)
            wot[k, :, 256 * e:256 * e + 256] = jnp.concatenate([wo[e, :, lanes], jnp.zeros((32, 1024), BF16)], axis=0).T

    arrived(statbuf, stat_sems.at[1])
    peaks, totals = statbuf[:, 0:4, :], statbuf[:, 4:8, :]
    factors = jnp.exp2((peaks - jnp.max(peaks, axis=0, keepdims=True)) * (scale * 1.4426950408889634))
    factors = factors / jnp.sum(factors * totals, axis=0, keepdims=True)
    factors = jnp.concatenate([factors.reshape(64, 128), jnp.zeros((64, 128), F32)], axis=0)
    wcol[...] = factors.T
    own_factors = wcol[pl.ds(pl.multiple_of(32 * group + 8 * y, 8), 8), :]
    own_factors = jnp.concatenate([own_factors, own_factors], axis=0)
    summed = []
    for i in range(4):
        arrived(rsbuf.at[i], rs_sems.at[1, i])
        acc = jnp.zeros((16, 256), F32)
        for d in range(16):
            acc = acc + own_factors[:, 4 * d + i:4 * d + i + 1] * rsbuf[i, d].astype(F32)
        summed.append(jnp.concatenate([acc[0:8], acc[8:16]], axis=1))
    summed = jnp.concatenate(summed, axis=0)
    high = summed.astype(BF16)
    low = (summed - high.astype(F32)).astype(BF16)
    both = jnp.concatenate([high, low], axis=0)
    uv_local.wait()
    own_row = lax.broadcasted_iota(jnp.int32, (32, 128), 0) % 8
    values = jnp.zeros((32, 128), F32)
    for h in range(0, 8, 2):
        product = nn(both, jnp.concatenate([uv[h], uv[h + 1]], axis=1))
        product = product[0:32] + product[32:64]
        values = jnp.where(own_row == h, product[:, 0:128], jnp.where(own_row == h + 1, product[:, 128:256], values))
    vmsg[...] = values.astype(BF16)

    for a, b in steps:
        device = (2 * (4 * ((z + a) % 4) + (y + b) % 4) + 1 - c, group)
        remote(vmsg, vbuf.at[y, x], v_sems.at[4], v_sems.at[y], device).start()
    head_terms = jnp.zeros((16, 512), F32)
    for k in range(4):
        from_y = (y + k) % 4
        arrived(vbuf.at[from_y], v_sems.at[from_y])
        vwide[k] = vbuf[from_y].astype(F32).reshape(128, 128)
        for h in range(0, 8, 2):
            rows = jnp.concatenate(
                [vwide[k, pl.ds(h, 16, stride=8), :], vwide[k, pl.ds(h + 1, 16, stride=8), :]], axis=1
            ).astype(BF16)
            head_terms = head_terms + nn(rows, wot[from_y, 128 * h:128 * h + 256, :])

    rows_c = lax.broadcasted_iota(jnp.int32, (8, 256), 0) // 4 == 1 - c
    for e in range(2):
        for k in range(4):
            term = head_terms[4 * k:4 * k + 4, 256 * e:256 * e + 256]
            terms[2 * k + e] = jnp.where(rows_c, jnp.concatenate([term, term], axis=0), 0.0)
    t_slot = 4 * c + x
    for to_x, to_c, device in across:
        remote(terms.at[2 * to_x + to_c], out.at[t_slot], t_sems.at[0], t_sems.at[1], device).start()
    pltpu.make_async_copy(terms.at[slot], out.at[t_slot], t_sems.at[1]).start()
    arrived(out, t_sems.at[1])

    for copy in rope_copies + twin_copies:
        copy.wait_send()
    pl.when(shift != 0)(uv_push.wait_send)
    arrived(ybuf.at[pl.ds(0, 7)], x_sems.at[0])
    for i in range(4):
        arrived(qbuf.at[i, pl.ds(0, 15)], q_sems.at[0, i])
        arrived(rsbuf.at[i, pl.ds(0, 15)], rs_sems.at[0, i])
    arrived(statbuf.at[pl.ds(0, 15)], stat_sems.at[0])
    arrived(vbuf, v_sems.at[4])
    arrived(terms.at[pl.ds(0, 7)], t_sems.at[0])


def body(q_nope, q_rope, latent_cache, rope_keys, lengths, w_uk, w_uv, w_out):
    any_spec = pl.BlockSpec(memory_space=pl.ANY)
    dma = pltpu.SemaphoreType.DMA
    terms = pl.pallas_call(
        kernel,
        out_shape=jax.ShapeDtypeStruct((8, 8, 256), F32),
        in_specs=[any_spec] * 8,
        out_specs=any_spec,
        scratch_shapes=[
            pltpu.VMEM((1024, 128), BF16),
            pltpu.VMEM((512, 128), BF16),
            pltpu.VMEM((8, 16, 128), BF16),
            pltpu.VMEM((8, 16, 128), BF16),
            pltpu.VMEM((4, 2, 16, 128), BF16),
            pltpu.VMEM((4, 16, 2, 16, 128), BF16),
            pltpu.VMEM((4, 4, 32, 64), BF16),
            pltpu.VMEM((4, 128, 1024), F32),
            pltpu.VMEM((4, 1024, 512), BF16),
            pltpu.VMEM((4, 64, 1024), BF16),
            pltpu.VMEM((8, 512, 128), BF16),
            pltpu.VMEM((2, 224, 4096), BF16),
            pltpu.VMEM((4, 512, 1024), BF16),
            pltpu.VMEM((4, 1024, 512), BF16),
            pltpu.VMEM((4, 16, 16, 256), BF16),
            pltpu.VMEM((8, 128), F32),
            pltpu.VMEM((4, 16, 16, 256), BF16),
            pltpu.VMEM((16, 8, 128), F32),
            pltpu.VMEM((128, 128), F32),
            pltpu.VMEM((32, 128), BF16),
            pltpu.VMEM((4, 4, 32, 128), BF16),
            pltpu.VMEM((4, 128, 128), F32),
            pltpu.VMEM((8, 8, 256), F32),
            dma((8,)), dma((2, 3)), dma((2, 3)), dma((2,)), dma((2, 4)), dma((2, 4)), dma((2,)), dma((5,)), dma((2,)), dma((2,)),
            pltpu.SemaphoreType.REGULAR,
            pltpu.SMEM((32,), jnp.int32),
        ],
        compiler_params=pltpu.CompilerParams(
            collective_id=0, has_side_effects=True, vmem_limit_bytes=48 << 20
        ),
    )(
        *(
            pltpu.with_memory_space_constraint(operand, pltpu.HBM)
            for operand in (
                lengths,
                q_nope.reshape(1024, 128),
                q_rope,
                latent_cache,
                jnp.swapaxes(rope_keys, 1, 2),
                jnp.swapaxes(w_uk, 1, 2).reshape(512, 128),
                w_uv,
                w_out.T,
            )
        )
    )
    return jnp.sum(terms, axis=0)[:, 0:224].astype(BF16)


def solution(mesh):
    return jax.shard_map(
        body,
        mesh=mesh,
        in_specs=(
            P(None, "head", None),
            P(None, "head", None),
            P(None, "ctx", None),
            P(None, "ctx", None),
            P(),
            P("head", None, "ctx"),
            P("head", None, None),
            P("head", "ctx"),
        ),
        out_specs=P("head", "ctx"),
        check_vma=False,
    )
```

```python
import functools

import jax
import jax.numpy as jnp
from jax import lax
from jax.experimental import pallas as pl
from jax.experimental.pallas import tpu as pltpu
from jax.sharding import PartitionSpec as P

MESH = pl.DeviceIdType.MESH
F32 = jnp.float32
BF16 = jnp.bfloat16


def nt(a, b):
    return lax.dot_general(a, b, (((1,), (1,)), ((), ())), preferred_element_type=F32)


def nn(a, b):
    return jnp.dot(a, b, preferred_element_type=F32)


def kernel(
    lengths_in, q_nope, q_rope, cache, keys, w_uk, w_uv, w_out, out,
    qn, wk, ybuf, xbuf, ebuf, qbuf, rbuf, base, cbuf, kbuf, uv, wo,
    ctbuf, wot, obuf, stat, rsbuf, statbuf, wcol, vmsg, vbuf, vwide, terms,
    load_sem, rope_sems, pair_sems, x_sems, q_sems, rs_sems, stat_sems, v_sems, t_sems, uv_sems, ready, lengths,
):
    ctx = lax.axis_index("ctx")
    x = lax.axis_index("head")
    chip, c = ctx // 2, ctx % 2
    z, y = chip // 4, chip % 4
    twin = ctx + 1 - 2 * c
    scale = (128 + 64) ** (-0.5)
    shift = (z + 2 * c) % 4
    group = (x + shift) % 4

    def remote(src, dst, send_sem, recv_sem, device):
        return pltpu.make_async_remote_copy(
            src_ref=src, dst_ref=dst, send_sem=send_sem, recv_sem=recv_sem, device_id=device, device_id_type=MESH
        )

    def arrived(ref, sem):
        pltpu.make_async_copy(ref, ref, sem).wait()

    across = []
    for k in range(1, 8):
        to_x, to_c = (x + k // 2) % 4, (c + k) % 2
        across.append((to_x, to_c, (2 * chip + to_c, to_x)))
    steps = [(a, b) for a in range(4) for b in range(4)]
    steps.sort(key=lambda s: -(min(s[0], 4 - s[0]) + min(s[1], 4 - s[1])))
    plane = [(2 * (4 * ((z + a) % 4) + (y + b) % 4) + c, x) for a, b in steps if (a, b) != (0, 0)]
    along_y = [(2 * (4 * z + (y + b) % 4) + c, x) for b in (2, 1, 3)]
    along_z = [(2 * (4 * ((z + a) % 4) + y) + c, x) for a in (2, 1, 3)]

    loads = [
        pltpu.make_async_copy(q_nope, qn, load_sem.at[0]),
        pltpu.make_async_copy(w_uk, wk, load_sem.at[1]),
    ]
    for load in loads:
        load.start()

    barrier = pltpu.get_barrier_semaphore()
    for device in along_y + along_z:
        pl.semaphore_signal(barrier, inc=1, device_id=device, device_id_type=MESH)
    for _, _, device in across:
        pl.semaphore_signal(barrier, inc=1, device_id=device, device_id_type=MESH)

    mine, theirs = 8 * x + 4 * c, 8 * x + 4 * (1 - c)
    half = pl.ds(pl.multiple_of(c * 512, 512), 512)
    twin_half = pl.ds(pl.multiple_of((1 - c) * 512, 512), 512)
    later = [
        pltpu.make_async_copy(cache.at[pl.ds(mine, 4)], cbuf.at[:, half], load_sem.at[2]),
        pltpu.make_async_copy(keys.at[pl.ds(mine, 4)], kbuf.at[:, :, half], load_sem.at[3]),
        pltpu.make_async_copy(w_out, wo.at[c], load_sem.at[5]),
        pltpu.make_async_copy(q_rope.at[pl.ds(mine, 4)], rbuf.at[x], load_sem.at[6]),
        pltpu.make_async_copy(lengths_in, lengths, load_sem.at[7]),
    ]
    for load in later:
        load.start()
    load_cache, load_keys, load_out, load_rope, load_lengths = later

    loads[0].wait()
    loads[1].wait()
    row_head = lax.broadcasted_iota(jnp.int32, (512, 128), 0) // 16
    lane_head = lax.broadcasted_iota(jnp.int32, (512, 128), 1) % 32
    own_head = row_head == lane_head
    for t in range(8):
        every = nt(wk[...], qn[pl.ds(128 * t, 128), :])
        kept = jnp.where(own_head, every, 0.0).reshape(32, 16, 128)
        ybuf[t] = jnp.sum(kept, axis=0).astype(BF16)

    pl.semaphore_wait(barrier, 13)

    slot = 2 * x + c
    for to_x, to_c, device in across:
        remote(ybuf.at[2 * to_x + to_c], xbuf.at[slot], x_sems.at[0], x_sems.at[1], device).start()
    pltpu.make_async_copy(ybuf.at[slot], xbuf.at[slot], x_sems.at[1]).start()
    for device in along_y:
        pl.semaphore_signal(ready, inc=1, device_id=device, device_id_type=MESH)
    rope_copies = []
    for k in range(1, 4):
        to = (x + k) % 4
        copy = remote(
            q_rope.at[pl.ds(8 * to + 4 * c, 4)], rbuf.at[x], rope_sems.at[0, k - 1], rope_sems.at[1, k - 1], (ctx, to)
        )
        copy.start()
        rope_copies.append(copy)
    twin_copies = [
        remote(cache.at[pl.ds(theirs, 4)], cbuf.at[:, half], pair_sems.at[0, 0], pair_sems.at[1, 0], (twin, x)),
        remote(keys.at[pl.ds(theirs, 4)], kbuf.at[:, :, half], pair_sems.at[0, 1], pair_sems.at[1, 1], (twin, x)),
        remote(w_out, wo.at[c], pair_sems.at[0, 2], pair_sems.at[1, 2], (twin, x)),
    ]
    twin_copies[0].start()
    twin_copies[1].start()
    heads = w_uv.at[pl.ds(8 * y, 8)]
    uv_local = pltpu.make_async_copy(heads, uv, uv_sems.at[1])
    uv_push = remote(heads, uv, uv_sems.at[0], uv_sems.at[1], (ctx, (x + 4 - shift) % 4))
    pl.when(shift == 0)(uv_local.start)
    pl.when(shift != 0)(uv_push.start)

    arrived(xbuf, x_sems.at[1])
    pl.semaphore_wait(ready, 3)
    for i in range(4):
        for e in range(2):
            ebuf[i, e] = jnp.concatenate([xbuf[2 * g + e, :, 32 * i:32 * i + 32] for g in range(4)], axis=1)
        for device in plane:
            remote(ebuf.at[i], qbuf.at[i, chip], q_sems.at[0, i], q_sems.at[1, i], device).start()
        pltpu.make_async_copy(ebuf.at[i], qbuf.at[i, chip], q_sems.at[1, i]).start()
    twin_copies[2].start()

    load_keys.wait()
    load_rope.wait()
    load_lengths.wait()
    twin_copies[1].wait_recv()
    for copy in rope_copies:
        copy.wait_recv()
    place = chip * 1024 + lax.broadcasted_iota(jnp.int32, (128, 1024), 1)
    for i in range(4):
        base[i] = jnp.where(place < lengths[mine + i], nn(rbuf[:, i].reshape(128, 64), kbuf[i]), -1e30)
    load_cache.wait()
    for i in range(4):
        ctbuf[i, :, half] = cbuf[i, half, :].T
    twin_copies[0].wait_recv()
    for i in range(4):
        ctbuf[i, :, twin_half] = cbuf[i, twin_half, :].T

    def scores_of(i):
        arrived(qbuf.at[i], q_sems.at[1, i])
        return nn(qbuf[i].reshape(512, 128).T, ctbuf[i]) + base[i]

    lane = lax.broadcasted_iota(jnp.int32, (128, 128), 1)
    stats = jnp.zeros((128, 128), F32)
    for i in range(4):
        scores = scores_of(i)
        peak = jnp.maximum(jnp.max(scores, axis=1, keepdims=True), -1e29)
        weights = jnp.exp2((scores - peak) * (scale * 1.4426950408889634))
        total = jnp.sum(weights, axis=1, keepdims=True)
        stats = jnp.where(lane == i, peak, jnp.where(lane == 4 + i, total, stats))
        if i == 3:
            stat[...] = stats.T[0:8, :]
            for device in plane:
                remote(stat, statbuf.at[chip], stat_sems.at[0], stat_sems.at[1], device).start()
            pltpu.make_async_copy(stat, statbuf.at[chip], stat_sems.at[1]).start()
        part = nn(weights.astype(BF16), cbuf[i]).reshape(16, 8, 512)
        obuf[i] = jnp.concatenate([part[:, :, 0:256], part[:, :, 256:512]], axis=1).astype(BF16)
        for a, b in steps:
            to_z, to_y = (z + a) % 4, (y + b) % 4
            source = obuf.at[i, 4 * ((x + to_z + 2 * c) % 4) + to_y]
            if (a, b) == (0, 0):
                pltpu.make_async_copy(source, rsbuf.at[i, chip], rs_sems.at[1, i]).start()
            else:
                device = (2 * (4 * to_z + to_y) + c, x)
                remote(source, rsbuf.at[i, chip], rs_sems.at[0, i], rs_sems.at[1, i], device).start()
    load_out.wait()
    twin_copies[2].wait_recv()
    for e in range(2):
        for k in range(4):
            lanes = slice(1024 * k, 1024 * k + 1024)
            wot[k, :, 256 * e:256 * e + 256] = jnp.concatenate([wo[e, :, lanes], jnp.zeros((32, 1024), BF16)], axis=0).T

    arrived(statbuf, stat_sems.at[1])
    peaks, totals = statbuf[:, 0:4, :], statbuf[:, 4:8, :]
    factors = jnp.exp2((peaks - jnp.max(peaks, axis=0, keepdims=True)) * (scale * 1.4426950408889634))
    factors = factors / jnp.sum(factors * totals, axis=0, keepdims=True)
    factors = jnp.concatenate([factors.reshape(64, 128), jnp.zeros((64, 128), F32)], axis=0)
    wcol[...] = factors.T
    own_factors = wcol[pl.ds(pl.multiple_of(32 * group + 8 * y, 8), 8), :]
    own_factors = jnp.concatenate([own_factors, own_factors], axis=0)
    summed = []
    for i in range(4):
        arrived(rsbuf.at[i], rs_sems.at[1, i])
        acc = jnp.zeros((16, 256), F32)
        for d in range(16):
            acc = acc + own_factors[:, 4 * d + i:4 * d + i + 1] * rsbuf[i, d].astype(F32)
        summed.append(jnp.concatenate([acc[0:8], acc[8:16]], axis=1))
    summed = jnp.concatenate(summed, axis=0)
    high = summed.astype(BF16)
    low = (summed - high.astype(F32)).astype(BF16)
    both = jnp.concatenate([high, low], axis=0)
    uv_local.wait()
    own_row = lax.broadcasted_iota(jnp.int32, (32, 128), 0) % 8
    values = jnp.zeros((32, 128), F32)
    for h in range(0, 8, 2):
        product = nn(both, jnp.concatenate([uv[h], uv[h + 1]], axis=1))
        product = product[0:32] + product[32:64]
        values = jnp.where(own_row == h, product[:, 0:128], jnp.where(own_row == h + 1, product[:, 128:256], values))
    vmsg[...] = values.astype(BF16)

    for a, b in steps:
        device = (2 * (4 * ((z + a) % 4) + (y + b) % 4) + 1 - c, group)
        remote(vmsg, vbuf.at[y, x], v_sems.at[4], v_sems.at[y], device).start()
    head_terms = jnp.zeros((16, 512), F32)
    for k in range(4):
        from_y = (y + k) % 4
        arrived(vbuf.at[from_y], v_sems.at[from_y])
        vwide[k] = vbuf[from_y].astype(F32).reshape(128, 128)
        for h in range(0, 8, 2):
            rows = jnp.concatenate(
                [vwide[k, pl.ds(h, 16, stride=8), :], vwide[k, pl.ds(h + 1, 16, stride=8), :]], axis=1
            ).astype(BF16)
            head_terms = head_terms + nn(rows, wot[from_y, 128 * h:128 * h + 256, :])

    rows_c = lax.broadcasted_iota(jnp.int32, (8, 256), 0) // 4 == 1 - c
    for e in range(2):
        for k in range(4):
            term = head_terms[4 * k:4 * k + 4, 256 * e:256 * e + 256]
            terms[2 * k + e] = jnp.where(rows_c, jnp.concatenate([term, term], axis=0), 0.0)
    t_slot = 4 * c + x
    for to_x, to_c, device in across:
        remote(terms.at[2 * to_x + to_c], out.at[t_slot], t_sems.at[0], t_sems.at[1], device).start()
    pltpu.make_async_copy(terms.at[slot], out.at[t_slot], t_sems.at[1]).start()
    arrived(out, t_sems.at[1])

    for copy in rope_copies + twin_copies:
        copy.wait_send()
    pl.when(shift != 0)(uv_push.wait_send)
    arrived(ybuf.at[pl.ds(0, 7)], x_sems.at[0])
    for i in range(4):
        arrived(qbuf.at[i, pl.ds(0, 15)], q_sems.at[0, i])
        arrived(rsbuf.at[i, pl.ds(0, 15)], rs_sems.at[0, i])
    arrived(statbuf.at[pl.ds(0, 15)], stat_sems.at[0])
    arrived(vbuf, v_sems.at[4])
    arrived(terms.at[pl.ds(0, 7)], t_sems.at[0])


def body(q_nope, q_rope, latent_cache, rope_keys, lengths, w_uk, w_uv, w_out):
    any_spec = pl.BlockSpec(memory_space=pl.ANY)
    dma = pltpu.SemaphoreType.DMA
    terms = pl.pallas_call(
        kernel,
        out_shape=jax.ShapeDtypeStruct((8, 8, 256), F32),
        in_specs=[any_spec] * 8,
        out_specs=any_spec,
        scratch_shapes=[
            pltpu.VMEM((1024, 128), BF16),
            pltpu.VMEM((512, 128), BF16),
            pltpu.VMEM((8, 16, 128), BF16),
            pltpu.VMEM((8, 16, 128), BF16),
            pltpu.VMEM((4, 2, 16, 128), BF16),
            pltpu.VMEM((4, 16, 2, 16, 128), BF16),
            pltpu.VMEM((4, 4, 32, 64), BF16),
            pltpu.VMEM((4, 128, 1024), F32),
            pltpu.VMEM((4, 1024, 512), BF16),
            pltpu.VMEM((4, 64, 1024), BF16),
            pltpu.VMEM((8, 512, 128), BF16),
            pltpu.VMEM((2, 224, 4096), BF16),
            pltpu.VMEM((4, 512, 1024), BF16),
            pltpu.VMEM((4, 1024, 512), BF16),
            pltpu.VMEM((4, 16, 16, 256), BF16),
            pltpu.VMEM((8, 128), F32),
            pltpu.VMEM((4, 16, 16, 256), BF16),
            pltpu.VMEM((16, 8, 128), F32),
            pltpu.VMEM((128, 128), F32),
            pltpu.VMEM((32, 128), BF16),
            pltpu.VMEM((4, 4, 32, 128), BF16),
            pltpu.VMEM((4, 128, 128), F32),
            pltpu.VMEM((8, 8, 256), F32),
            dma((8,)), dma((2, 3)), dma((2, 3)), dma((2,)), dma((2, 4)), dma((2, 4)), dma((2,)), dma((5,)), dma((2,)), dma((2,)),
            pltpu.SemaphoreType.REGULAR,
            pltpu.SMEM((32,), jnp.int32),
        ],
        compiler_params=pltpu.CompilerParams(
            collective_id=0, has_side_effects=True, vmem_limit_bytes=48 << 20
        ),
    )(
        *(
            pltpu.with_memory_space_constraint(operand, pltpu.HBM)
            for operand in (
                lengths,
                q_nope.reshape(1024, 128),
                q_rope,
                latent_cache,
                jnp.swapaxes(rope_keys, 1, 2),
                jnp.swapaxes(w_uk, 1, 2).reshape(512, 128),
                w_uv,
                w_out.T,
            )
        )
    )
    return jnp.sum(terms, axis=0)[:, 0:224].astype(BF16)


def solution(mesh):
    return jax.shard_map(
        body,
        mesh=mesh,
        in_specs=(
            P(None, "head", None),
            P(None, "head", None),
            P(None, "ctx", None),
            P(None, "ctx", None),
            P(),
            P("head", None, "ctx"),
            P("head", None, None),
            P("head", "ctx"),
        ),
        out_specs=P("head", "ctx"),
        check_vma=False,
    )
```

```python
import functools

import jax
import jax.numpy as jnp
from jax import lax
from jax.experimental import pallas as pl
from jax.experimental.pallas import tpu as pltpu
from jax.sharding import PartitionSpec as P

MESH = pl.DeviceIdType.MESH
F32 = jnp.float32
BF16 = jnp.bfloat16


def nt(a, b):
    return lax.dot_general(a, b, (((1,), (1,)), ((), ())), preferred_element_type=F32)


def nn(a, b):
    return jnp.dot(a, b, preferred_element_type=F32)


def kernel(
    lengths_in, q_nope, q_rope, cache, keys, w_uk, w_uv, w_out, out,
    qn, wk, ybuf, xbuf, ebuf, qbuf, rbuf, base, cbuf, kbuf, uv, wo,
    ctbuf, wot, obuf, stat, rsbuf, statbuf, wcol, vmsg, vbuf, vwide, terms,
    load_sem, rope_sems, pair_sems, x_sems, q_sems, rs_sems, stat_sems, v_sems, t_sems, uv_sems, ready, lengths,
):
    ctx = lax.axis_index("ctx")
    x = lax.axis_index("head")
    chip, c = ctx // 2, ctx % 2
    z, y = chip // 4, chip % 4
    twin = ctx + 1 - 2 * c
    scale = (128 + 64) ** (-0.5)
    shift = (z + 2 * c) % 4
    group = (x + shift) % 4

    def remote(src, dst, send_sem, recv_sem, device):
        return pltpu.make_async_remote_copy(
            src_ref=src, dst_ref=dst, send_sem=send_sem, recv_sem=recv_sem, device_id=device, device_id_type=MESH
        )

    def arrived(ref, sem):
        pltpu.make_async_copy(ref, ref, sem).wait()

    across = []
    for k in (4, 5, 2, 3, 6, 7, 1):
        to_x, to_c = (x + k // 2) % 4, (c + k) % 2
        across.append((to_x, to_c, (2 * chip + to_c, to_x)))
    steps = [(a, b) for a in range(4) for b in range(4)]
    steps.sort(key=lambda s: -(min(s[0], 4 - s[0]) + min(s[1], 4 - s[1])))
    plane = [(2 * (4 * ((z + a) % 4) + (y + b) % 4) + c, x) for a, b in steps if (a, b) != (0, 0)]
    along_y = [(2 * (4 * z + (y + b) % 4) + c, x) for b in (2, 1, 3)]
    along_z = [(2 * (4 * ((z + a) % 4) + y) + c, x) for a in (2, 1, 3)]

    loads = [
        pltpu.make_async_copy(q_nope, qn, load_sem.at[0]),
        pltpu.make_async_copy(w_uk, wk, load_sem.at[1]),
    ]
    for load in loads:
        load.start()

    barrier = pltpu.get_barrier_semaphore()
    for device in along_y + along_z:
        pl.semaphore_signal(barrier, inc=1, device_id=device, device_id_type=MESH)
    for _, _, device in across:
        pl.semaphore_signal(barrier, inc=1, device_id=device, device_id_type=MESH)

    mine, theirs = 8 * x + 4 * c, 8 * x + 4 * (1 - c)
    half = pl.ds(pl.multiple_of(c * 512, 512), 512)
    twin_half = pl.ds(pl.multiple_of((1 - c) * 512, 512), 512)
    later = [
        pltpu.make_async_copy(cache.at[pl.ds(mine, 4)], cbuf.at[:, half], load_sem.at[2]),
        pltpu.make_async_copy(keys.at[pl.ds(mine, 4)], kbuf.at[:, :, half], load_sem.at[3]),
        pltpu.make_async_copy(w_out, wo.at[c], load_sem.at[5]),
        pltpu.make_async_copy(q_rope.at[pl.ds(mine, 4)], rbuf.at[x], load_sem.at[6]),
        pltpu.make_async_copy(lengths_in, lengths, load_sem.at[7]),
    ]
    for load in later:
        load.start()
    load_cache, load_keys, load_out, load_rope, load_lengths = later

    loads[0].wait()
    loads[1].wait()
    row_head = lax.broadcasted_iota(jnp.int32, (512, 128), 0) // 16
    lane_head = lax.broadcasted_iota(jnp.int32, (512, 128), 1) % 32
    own_head = row_head == lane_head
    for t in range(8):
        every = nt(wk[...], qn[pl.ds(128 * t, 128), :])
        kept = jnp.where(own_head, every, 0.0).reshape(32, 16, 128)
        ybuf[t] = jnp.sum(kept, axis=0).astype(BF16)

    pl.semaphore_wait(barrier, 13)

    slot = 2 * x + c
    for to_x, to_c, device in across:
        remote(ybuf.at[2 * to_x + to_c], xbuf.at[slot], x_sems.at[0], x_sems.at[1], device).start()
    pltpu.make_async_copy(ybuf.at[slot], xbuf.at[slot], x_sems.at[1]).start()
    for device in along_y:
        pl.semaphore_signal(ready, inc=1, device_id=device, device_id_type=MESH)
    rope_copies = []
    for k in range(1, 4):
        to = (x + k) % 4
        copy = remote(
            q_rope.at[pl.ds(8 * to + 4 * c, 4)], rbuf.at[x], rope_sems.at[0, k - 1], rope_sems.at[1, k - 1], (ctx, to)
        )
        copy.start()
        rope_copies.append(copy)
    twin_copies = [
        remote(cache.at[pl.ds(theirs, 4)], cbuf.at[:, half], pair_sems.at[0, 0], pair_sems.at[1, 0], (twin, x)),
        remote(keys.at[pl.ds(theirs, 4)], kbuf.at[:, :, half], pair_sems.at[0, 1], pair_sems.at[1, 1], (twin, x)),
        remote(w_out, wo.at[c], pair_sems.at[0, 2], pair_sems.at[1, 2], (twin, x)),
    ]
    twin_copies[0].start()
    twin_copies[1].start()
    heads = w_uv.at[pl.ds(8 * y, 8)]
    uv_local = pltpu.make_async_copy(heads, uv, uv_sems.at[1])
    uv_push = remote(heads, uv, uv_sems.at[0], uv_sems.at[1], (ctx, (x + 4 - shift) % 4))
    pl.when(shift == 0)(uv_local.start)
    pl.when(shift != 0)(uv_push.start)

    arrived(xbuf, x_sems.at[1])
    pl.semaphore_wait(ready, 3)
    for i in range(4):
        for e in range(2):
            ebuf[i, e] = jnp.concatenate([xbuf[2 * g + e, :, 32 * i:32 * i + 32] for g in range(4)], axis=1)
        for device in plane:
            remote(ebuf.at[i], qbuf.at[i, chip], q_sems.at[0, i], q_sems.at[1, i], device).start()
        pltpu.make_async_copy(ebuf.at[i], qbuf.at[i, chip], q_sems.at[1, i]).start()
    twin_copies[2].start()

    load_keys.wait()
    load_rope.wait()
    load_lengths.wait()
    twin_copies[1].wait_recv()
    for copy in rope_copies:
        copy.wait_recv()
    place = chip * 1024 + lax.broadcasted_iota(jnp.int32, (128, 1024), 1)
    for i in range(4):
        base[i] = jnp.where(place < lengths[mine + i], nn(rbuf[:, i].reshape(128, 64), kbuf[i]), -1e30)
    load_cache.wait()
    for i in range(4):
        ctbuf[i, :, half] = cbuf[i, half, :].T
    twin_copies[0].wait_recv()
    for i in range(4):
        ctbuf[i, :, twin_half] = cbuf[i, twin_half, :].T

    def scores_of(i):
        arrived(qbuf.at[i], q_sems.at[1, i])
        return nn(qbuf[i].reshape(512, 128).T, ctbuf[i]) + base[i]

    lane = lax.broadcasted_iota(jnp.int32, (128, 128), 1)
    stats = jnp.zeros((128, 128), F32)
    for i in range(4):
        scores = scores_of(i)
        peak = jnp.maximum(jnp.max(scores, axis=1, keepdims=True), -1e29)
        weights = jnp.exp2((scores - peak) * (scale * 1.4426950408889634))
        total = jnp.sum(weights, axis=1, keepdims=True)
        stats = jnp.where(lane == i, peak, jnp.where(lane == 4 + i, total, stats))
        if i == 3:
            stat[...] = stats.T[0:8, :]
            for device in plane:
                remote(stat, statbuf.at[chip], stat_sems.at[0], stat_sems.at[1], device).start()
            pltpu.make_async_copy(stat, statbuf.at[chip], stat_sems.at[1]).start()
        part = nn(weights.astype(BF16), cbuf[i]).reshape(16, 8, 512)
        obuf[i] = jnp.concatenate([part[:, :, 0:256], part[:, :, 256:512]], axis=1).astype(BF16)
        for a, b in steps:
            to_z, to_y = (z + a) % 4, (y + b) % 4
            source = obuf.at[i, 4 * ((x + to_z + 2 * c) % 4) + to_y]
            if (a, b) == (0, 0):
                pltpu.make_async_copy(source, rsbuf.at[i, chip], rs_sems.at[1, i]).start()
            else:
                device = (2 * (4 * to_z + to_y) + c, x)
                remote(source, rsbuf.at[i, chip], rs_sems.at[0, i], rs_sems.at[1, i], device).start()
    load_out.wait()
    twin_copies[2].wait_recv()
    for e in range(2):
        for k in range(4):
            lanes = slice(1024 * k, 1024 * k + 1024)
            wot[k, :, 256 * e:256 * e + 256] = jnp.concatenate([wo[e, :, lanes], jnp.zeros((32, 1024), BF16)], axis=0).T

    arrived(statbuf, stat_sems.at[1])
    peaks, totals = statbuf[:, 0:4, :], statbuf[:, 4:8, :]
    factors = jnp.exp2((peaks - jnp.max(peaks, axis=0, keepdims=True)) * (scale * 1.4426950408889634))
    factors = factors / jnp.sum(factors * totals, axis=0, keepdims=True)
    factors = jnp.concatenate([factors.reshape(64, 128), jnp.zeros((64, 128), F32)], axis=0)
    wcol[...] = factors.T
    own_factors = wcol[pl.ds(pl.multiple_of(32 * group + 8 * y, 8), 8), :]
    own_factors = jnp.concatenate([own_factors, own_factors], axis=0)
    summed = []
    for i in range(4):
        arrived(rsbuf.at[i], rs_sems.at[1, i])
        acc = jnp.zeros((16, 256), F32)
        for d in range(16):
            acc = acc + own_factors[:, 4 * d + i:4 * d + i + 1] * rsbuf[i, d].astype(F32)
        summed.append(jnp.concatenate([acc[0:8], acc[8:16]], axis=1))
    summed = jnp.concatenate(summed, axis=0)
    high = summed.astype(BF16)
    low = (summed - high.astype(F32)).astype(BF16)
    both = jnp.concatenate([high, low], axis=0)
    uv_local.wait()
    own_row = lax.broadcasted_iota(jnp.int32, (32, 128), 0) % 8
    values = jnp.zeros((32, 128), F32)
    for h in range(0, 8, 2):
        product = nn(both, jnp.concatenate([uv[h], uv[h + 1]], axis=1))
        product = product[0:32] + product[32:64]
        values = jnp.where(own_row == h, product[:, 0:128], jnp.where(own_row == h + 1, product[:, 128:256], values))
    vmsg[...] = values.astype(BF16)

    for a, b in steps:
        device = (2 * (4 * ((z + a) % 4) + (y + b) % 4) + 1 - c, group)
        remote(vmsg, vbuf.at[y, x], v_sems.at[4], v_sems.at[y], device).start()
    head_terms = jnp.zeros((16, 512), F32)
    for k in range(4):
        from_y = (y + k) % 4
        arrived(vbuf.at[from_y], v_sems.at[from_y])
        vwide[k] = vbuf[from_y].astype(F32).reshape(128, 128)
        for h in range(0, 8, 2):
            rows = jnp.concatenate(
                [vwide[k, pl.ds(h, 16, stride=8), :], vwide[k, pl.ds(h + 1, 16, stride=8), :]], axis=1
            ).astype(BF16)
            head_terms = head_terms + nn(rows, wot[from_y, 128 * h:128 * h + 256, :])

    rows_c = lax.broadcasted_iota(jnp.int32, (8, 256), 0) // 4 == 1 - c
    for e in range(2):
        for k in range(4):
            term = head_terms[4 * k:4 * k + 4, 256 * e:256 * e + 256]
            terms[2 * k + e] = jnp.where(rows_c, jnp.concatenate([term, term], axis=0), 0.0)
    t_slot = 4 * c + x
    for to_x, to_c, device in across:
        remote(terms.at[2 * to_x + to_c], out.at[t_slot], t_sems.at[0], t_sems.at[1], device).start()
    pltpu.make_async_copy(terms.at[slot], out.at[t_slot], t_sems.at[1]).start()
    for copy in rope_copies + twin_copies:
        copy.wait_send()
    pl.when(shift != 0)(uv_push.wait_send)
    arrived(ybuf.at[pl.ds(0, 7)], x_sems.at[0])
    for i in range(4):
        arrived(qbuf.at[i, pl.ds(0, 15)], q_sems.at[0, i])
        arrived(rsbuf.at[i, pl.ds(0, 15)], rs_sems.at[0, i])
    arrived(statbuf.at[pl.ds(0, 15)], stat_sems.at[0])
    arrived(vbuf, v_sems.at[4])
    arrived(terms.at[pl.ds(0, 7)], t_sems.at[0])
    arrived(out, t_sems.at[1])


def body(q_nope, q_rope, latent_cache, rope_keys, lengths, w_uk, w_uv, w_out):
    any_spec = pl.BlockSpec(memory_space=pl.ANY)
    dma = pltpu.SemaphoreType.DMA
    terms = pl.pallas_call(
        kernel,
        out_shape=jax.ShapeDtypeStruct((8, 8, 256), F32),
        in_specs=[any_spec] * 8,
        out_specs=any_spec,
        scratch_shapes=[
            pltpu.VMEM((1024, 128), BF16),
            pltpu.VMEM((512, 128), BF16),
            pltpu.VMEM((8, 16, 128), BF16),
            pltpu.VMEM((8, 16, 128), BF16),
            pltpu.VMEM((4, 2, 16, 128), BF16),
            pltpu.VMEM((4, 16, 2, 16, 128), BF16),
            pltpu.VMEM((4, 4, 32, 64), BF16),
            pltpu.VMEM((4, 128, 1024), F32),
            pltpu.VMEM((4, 1024, 512), BF16),
            pltpu.VMEM((4, 64, 1024), BF16),
            pltpu.VMEM((8, 512, 128), BF16),
            pltpu.VMEM((2, 224, 4096), BF16),
            pltpu.VMEM((4, 512, 1024), BF16),
            pltpu.VMEM((4, 1024, 512), BF16),
            pltpu.VMEM((4, 16, 16, 256), BF16),
            pltpu.VMEM((8, 128), F32),
            pltpu.VMEM((4, 16, 16, 256), BF16),
            pltpu.VMEM((16, 8, 128), F32),
            pltpu.VMEM((128, 128), F32),
            pltpu.VMEM((32, 128), BF16),
            pltpu.VMEM((4, 4, 32, 128), BF16),
            pltpu.VMEM((4, 128, 128), F32),
            pltpu.VMEM((8, 8, 256), F32),
            dma((8,)), dma((2, 3)), dma((2, 3)), dma((2,)), dma((2, 4)), dma((2, 4)), dma((2,)), dma((5,)), dma((2,)), dma((2,)),
            pltpu.SemaphoreType.REGULAR,
            pltpu.SMEM((32,), jnp.int32),
        ],
        compiler_params=pltpu.CompilerParams(
            collective_id=0, has_side_effects=True, vmem_limit_bytes=48 << 20
        ),
    )(
        *(
            pltpu.with_memory_space_constraint(operand, pltpu.HBM)
            for operand in (
                lengths,
                q_nope.reshape(1024, 128),
                q_rope,
                latent_cache,
                jnp.swapaxes(rope_keys, 1, 2),
                jnp.swapaxes(w_uk, 1, 2).reshape(512, 128),
                w_uv,
                w_out.T,
            )
        )
    )
    return jnp.sum(terms, axis=0)[:, 0:224].astype(BF16)


def solution(mesh):
    return jax.shard_map(
        body,
        mesh=mesh,
        in_specs=(
            P(None, "head", None),
            P(None, "head", None),
            P(None, "ctx", None),
            P(None, "ctx", None),
            P(),
            P("head", None, "ctx"),
            P("head", None, None),
            P("head", "ctx"),
        ),
        out_specs=P("head", "ctx"),
        check_vma=False,
    )
```

```python
import functools

import jax
import jax.numpy as jnp
from jax import lax
from jax.experimental import pallas as pl
from jax.experimental.pallas import tpu as pltpu
from jax.sharding import PartitionSpec as P

MESH = pl.DeviceIdType.MESH
F32 = jnp.float32
BF16 = jnp.bfloat16


def nt(a, b):
    return lax.dot_general(a, b, (((1,), (1,)), ((), ())), preferred_element_type=F32)


def nn(a, b):
    return jnp.dot(a, b, preferred_element_type=F32)


def kernel(
    lengths_in, q_nope, q_rope, cache, keys, w_uk, w_uv, w_out, out,
    qn, wk, ybuf, xbuf, ebuf, qbuf, rbuf, base, cbuf, kbuf, uv, wo,
    ctbuf, wot, obuf, stat, rsbuf, statbuf, wcol, vmsg, vbuf, vwide, terms,
    load_sem, rope_sems, pair_sems, x_sems, q_sems, rs_sems, stat_sems, v_sems, t_sems, uv_sems, ready, lengths,
):
    ctx = lax.axis_index("ctx")
    x = lax.axis_index("head")
    chip, c = ctx // 2, ctx % 2
    z, y = chip // 4, chip % 4
    twin = ctx + 1 - 2 * c
    scale = (128 + 64) ** (-0.5)
    shift = (z + 2 * c) % 4
    group = (x + shift) % 4

    def remote(src, dst, send_sem, recv_sem, device):
        return pltpu.make_async_remote_copy(
            src_ref=src, dst_ref=dst, send_sem=send_sem, recv_sem=recv_sem, device_id=device, device_id_type=MESH
        )

    def arrived(ref, sem):
        pltpu.make_async_copy(ref, ref, sem).wait()

    across = []
    for k in (4, 5, 2, 3, 6, 7, 1):
        to_x, to_c = (x + k // 2) % 4, (c + k) % 2
        across.append((to_x, to_c, (2 * chip + to_c, to_x)))
    steps = [(a, b) for a in range(4) for b in range(4)]
    steps.sort(key=lambda s: -(min(s[0], 4 - s[0]) + min(s[1], 4 - s[1])))
    plane = [(2 * (4 * ((z + a) % 4) + (y + b) % 4) + c, x) for a, b in steps if (a, b) != (0, 0)]
    along_y = [(2 * (4 * z + (y + b) % 4) + c, x) for b in (2, 1, 3)]
    along_z = [(2 * (4 * ((z + a) % 4) + y) + c, x) for a in (2, 1, 3)]

    loads = [
        pltpu.make_async_copy(q_nope, qn, load_sem.at[0]),
        pltpu.make_async_copy(w_uk, wk, load_sem.at[1]),
    ]
    for load in loads:
        load.start()

    barrier = pltpu.get_barrier_semaphore()
    for device in along_y + along_z:
        pl.semaphore_signal(barrier, inc=1, device_id=device, device_id_type=MESH)
    for _, _, device in across:
        pl.semaphore_signal(barrier, inc=1, device_id=device, device_id_type=MESH)

    mine, theirs = 8 * x + 4 * c, 8 * x + 4 * (1 - c)
    half = pl.ds(pl.multiple_of(c * 512, 512), 512)
    twin_half = pl.ds(pl.multiple_of((1 - c) * 512, 512), 512)
    later = [
        pltpu.make_async_copy(cache.at[pl.ds(mine, 4)], cbuf.at[:, half], load_sem.at[2]),
        pltpu.make_async_copy(keys.at[pl.ds(mine, 4)], kbuf.at[:, :, half], load_sem.at[3]),
        pltpu.make_async_copy(w_out, wo.at[c], load_sem.at[5]),
        pltpu.make_async_copy(q_rope.at[pl.ds(mine, 4)], rbuf.at[x], load_sem.at[6]),
        pltpu.make_async_copy(lengths_in, lengths, load_sem.at[7]),
    ]
    for load in later:
        load.start()
    load_cache, load_keys, load_out, load_rope, load_lengths = later

    loads[0].wait()
    loads[1].wait()
    row_head = lax.broadcasted_iota(jnp.int32, (512, 128), 0) // 16
    lane_head = lax.broadcasted_iota(jnp.int32, (512, 128), 1) % 32
    own_head = row_head == lane_head
    for t in range(8):
        every = nt(wk[...], qn[pl.ds(128 * t, 128), :])
        kept = jnp.where(own_head, every, 0.0).reshape(32, 16, 128)
        ybuf[t] = jnp.sum(kept, axis=0).astype(BF16)

    pl.semaphore_wait(barrier, 13)

    slot = 2 * x + c
    for to_x, to_c, device in across:
        remote(ybuf.at[2 * to_x + to_c], xbuf.at[slot], x_sems.at[0], x_sems.at[1], device).start()
    pltpu.make_async_copy(ybuf.at[slot], xbuf.at[slot], x_sems.at[1]).start()
    for device in along_y:
        pl.semaphore_signal(ready, inc=1, device_id=device, device_id_type=MESH)
    rope_copies = []
    for k in range(1, 4):
        to = (x + k) % 4
        copy = remote(
            q_rope.at[pl.ds(8 * to + 4 * c, 4)], rbuf.at[x], rope_sems.at[0, k - 1], rope_sems.at[1, k - 1], (ctx, to)
        )
        copy.start()
        rope_copies.append(copy)
    twin_copies = [
        remote(cache.at[pl.ds(theirs, 4)], cbuf.at[:, half], pair_sems.at[0, 0], pair_sems.at[1, 0], (twin, x)),
        remote(keys.at[pl.ds(theirs, 4)], kbuf.at[:, :, half], pair_sems.at[0, 1], pair_sems.at[1, 1], (twin, x)),
        remote(w_out, wo.at[c], pair_sems.at[0, 2], pair_sems.at[1, 2], (twin, x)),
    ]
    twin_copies[0].start()
    twin_copies[1].start()
    heads = w_uv.at[pl.ds(8 * y, 8)]
    uv_local = pltpu.make_async_copy(heads, uv, uv_sems.at[1])
    uv_push = remote(heads, uv, uv_sems.at[0], uv_sems.at[1], (ctx, (x + 4 - shift) % 4))
    pl.when(shift == 0)(uv_local.start)
    pl.when(shift != 0)(uv_push.start)

    arrived(xbuf, x_sems.at[1])
    pl.semaphore_wait(ready, 3)
    for i in range(4):
        for e in range(2):
            ebuf[i, e] = jnp.concatenate([xbuf[2 * g + e, :, 32 * i:32 * i + 32] for g in range(4)], axis=1)
        for device in plane:
            remote(ebuf.at[i], qbuf.at[i, chip], q_sems.at[0, i], q_sems.at[1, i], device).start()
        pltpu.make_async_copy(ebuf.at[i], qbuf.at[i, chip], q_sems.at[1, i]).start()
    twin_copies[2].start()

    load_keys.wait()
    load_rope.wait()
    load_lengths.wait()
    twin_copies[1].wait_recv()
    for copy in rope_copies:
        copy.wait_recv()
    place = chip * 1024 + lax.broadcasted_iota(jnp.int32, (128, 1024), 1)
    for i in range(4):
        base[i] = jnp.where(place < lengths[mine + i], nn(rbuf[:, i].reshape(128, 64), kbuf[i]), -1e30)
    load_cache.wait()
    for i in range(4):
        ctbuf[i, :, half] = cbuf[i, half, :].T
    twin_copies[0].wait_recv()
    for i in range(4):
        ctbuf[i, :, twin_half] = cbuf[i, twin_half, :].T

    def scores_of(i):
        arrived(qbuf.at[i], q_sems.at[1, i])
        return nn(qbuf[i].reshape(512, 128).T, ctbuf[i]) + base[i]

    lane = lax.broadcasted_iota(jnp.int32, (128, 128), 1)
    stats = jnp.zeros((128, 128), F32)
    for i in range(4):
        scores = scores_of(i)
        peak = jnp.maximum(jnp.max(scores, axis=1, keepdims=True), -1e29)
        weights = jnp.exp2((scores - peak) * (scale * 1.4426950408889634))
        total = jnp.sum(weights, axis=1, keepdims=True)
        stats = jnp.where(lane == i, peak, jnp.where(lane == 4 + i, total, stats))
        if i == 3:
            stat[...] = stats.T[0:8, :]
            for device in plane:
                remote(stat, statbuf.at[chip], stat_sems.at[0], stat_sems.at[1], device).start()
            pltpu.make_async_copy(stat, statbuf.at[chip], stat_sems.at[1]).start()
        part = nn(weights.astype(BF16), cbuf[i]).reshape(16, 8, 512)
        obuf[i] = jnp.concatenate([part[:, :, 0:256], part[:, :, 256:512]], axis=1).astype(BF16)
        for a, b in steps:
            to_z, to_y = (z + a) % 4, (y + b) % 4
            source = obuf.at[i, 4 * ((x + to_z + 2 * c) % 4) + to_y]
            if (a, b) == (0, 0):
                pltpu.make_async_copy(source, rsbuf.at[i, chip], rs_sems.at[1, i]).start()
            else:
                device = (2 * (4 * to_z + to_y) + c, x)
                remote(source, rsbuf.at[i, chip], rs_sems.at[0, i], rs_sems.at[1, i], device).start()
    load_out.wait()
    twin_copies[2].wait_recv()
    for e in range(2):
        for k in range(4):
            lanes = slice(1024 * k, 1024 * k + 1024)
            wot[k, :, 256 * e:256 * e + 256] = jnp.concatenate([wo[e, :, lanes], jnp.zeros((32, 1024), BF16)], axis=0).T

    arrived(statbuf, stat_sems.at[1])
    peaks, totals = statbuf[:, 0:4, :], statbuf[:, 4:8, :]
    factors = jnp.exp2((peaks - jnp.max(peaks, axis=0, keepdims=True)) * (scale * 1.4426950408889634))
    factors = factors / jnp.sum(factors * totals, axis=0, keepdims=True)
    factors = jnp.concatenate([factors.reshape(64, 128), jnp.zeros((64, 128), F32)], axis=0)
    wcol[...] = factors.T
    own_factors = wcol[pl.ds(pl.multiple_of(32 * group + 8 * y, 8), 8), :]
    own_factors = jnp.concatenate([own_factors, own_factors], axis=0)
    summed = []
    for i in range(4):
        arrived(rsbuf.at[i], rs_sems.at[1, i])
        acc = jnp.zeros((16, 256), F32)
        for d in range(16):
            acc = acc + own_factors[:, 4 * d + i:4 * d + i + 1] * rsbuf[i, d].astype(F32)
        summed.append(jnp.concatenate([acc[0:8], acc[8:16]], axis=1))
    summed = jnp.concatenate(summed, axis=0)
    high = summed.astype(BF16)
    low = (summed - high.astype(F32)).astype(BF16)
    both = jnp.concatenate([high, low], axis=0)
    uv_local.wait()
    own_row = lax.broadcasted_iota(jnp.int32, (32, 128), 0) % 8
    values = jnp.zeros((32, 128), F32)
    for h in range(0, 8, 2):
        product = nn(both, jnp.concatenate([uv[h], uv[h + 1]], axis=1))
        product = product[0:32] + product[32:64]
        values = jnp.where(own_row == h, product[:, 0:128], jnp.where(own_row == h + 1, product[:, 128:256], values))
    vmsg[...] = values.astype(BF16)

    for a, b in steps:
        device = (2 * (4 * ((z + a) % 4) + (y + b) % 4) + 1 - c, group)
        remote(vmsg, vbuf.at[y, x], v_sems.at[4], v_sems.at[y], device).start()
    head_terms = jnp.zeros((16, 512), F32)
    for k in range(4):
        from_y = (y + k) % 4
        arrived(vbuf.at[from_y], v_sems.at[from_y])
        vwide[k, 0:128] = vbuf[from_y].astype(F32).reshape(128, 128)
        for h in range(0, 8, 2):
            rows = jnp.concatenate(
                [vwide[k, pl.ds(h, 16, stride=8), :], vwide[k, pl.ds(h + 1, 16, stride=8), :]], axis=1
            ).astype(BF16)
            head_terms = head_terms + nn(rows, wot[from_y, 128 * h:128 * h + 256, :])

    rows_c = lax.broadcasted_iota(jnp.int32, (8, 256), 0) // 4 == 1 - c
    for e in range(2):
        for k in range(4):
            term = head_terms[4 * k:4 * k + 4, 256 * e:256 * e + 256]
            terms[2 * k + e] = jnp.where(rows_c, jnp.concatenate([term, term], axis=0), 0.0)
    t_slot = 4 * c + x
    for to_x, to_c, device in across:
        remote(terms.at[2 * to_x + to_c], out.at[t_slot], t_sems.at[0], t_sems.at[1], device).start()
    pltpu.make_async_copy(terms.at[slot], out.at[t_slot], t_sems.at[1]).start()
    for copy in rope_copies + twin_copies:
        copy.wait_send()
    pl.when(shift != 0)(uv_push.wait_send)
    arrived(ybuf.at[pl.ds(0, 7)], x_sems.at[0])
    for i in range(4):
        arrived(qbuf.at[i, pl.ds(0, 15)], q_sems.at[0, i])
        arrived(rsbuf.at[i, pl.ds(0, 15)], rs_sems.at[0, i])
    arrived(statbuf.at[pl.ds(0, 15)], stat_sems.at[0])
    arrived(vbuf, v_sems.at[4])
    arrived(terms.at[pl.ds(0, 7)], t_sems.at[0])
    arrived(out, t_sems.at[1])


def body(q_nope, q_rope, latent_cache, rope_keys, lengths, w_uk, w_uv, w_out):
    any_spec = pl.BlockSpec(memory_space=pl.ANY)
    dma = pltpu.SemaphoreType.DMA
    terms = pl.pallas_call(
        kernel,
        out_shape=jax.ShapeDtypeStruct((8, 8, 256), F32),
        in_specs=[any_spec] * 8,
        out_specs=any_spec,
        scratch_shapes=[
            pltpu.VMEM((1024, 128), BF16),
            pltpu.VMEM((512, 128), BF16),
            pltpu.VMEM((8, 16, 128), BF16),
            pltpu.VMEM((8, 16, 128), BF16),
            pltpu.VMEM((4, 2, 16, 128), BF16),
            pltpu.VMEM((4, 16, 2, 16, 128), BF16),
            pltpu.VMEM((4, 4, 32, 64), BF16),
            pltpu.VMEM((4, 128, 1024), F32),
            pltpu.VMEM((4, 1024, 512), BF16),
            pltpu.VMEM((4, 64, 1024), BF16),
            pltpu.VMEM((8, 512, 128), BF16),
            pltpu.VMEM((2, 224, 4096), BF16),
            pltpu.VMEM((4, 512, 1024), BF16),
            pltpu.VMEM((4, 1024, 512), BF16),
            pltpu.VMEM((4, 16, 16, 256), BF16),
            pltpu.VMEM((8, 128), F32),
            pltpu.VMEM((4, 16, 16, 256), BF16),
            pltpu.VMEM((16, 8, 128), F32),
            pltpu.VMEM((128, 128), F32),
            pltpu.VMEM((32, 128), BF16),
            pltpu.VMEM((4, 4, 32, 128), BF16),
            pltpu.VMEM((4, 136, 128), F32),
            pltpu.VMEM((8, 8, 256), F32),
            dma((8,)), dma((2, 3)), dma((2, 3)), dma((2,)), dma((2, 4)), dma((2, 4)), dma((2,)), dma((5,)), dma((2,)), dma((2,)),
            pltpu.SemaphoreType.REGULAR,
            pltpu.SMEM((32,), jnp.int32),
        ],
        compiler_params=pltpu.CompilerParams(
            collective_id=0, has_side_effects=True, vmem_limit_bytes=48 << 20
        ),
    )(
        *(
            pltpu.with_memory_space_constraint(operand, pltpu.HBM)
            for operand in (
                lengths,
                q_nope.reshape(1024, 128),
                q_rope,
                latent_cache,
                jnp.swapaxes(rope_keys, 1, 2),
                jnp.swapaxes(w_uk, 1, 2).reshape(512, 128),
                w_uv,
                w_out.T,
            )
        )
    )
    return jnp.sum(terms, axis=0)[:, 0:224].astype(BF16)


def solution(mesh):
    return jax.shard_map(
        body,
        mesh=mesh,
        in_specs=(
            P(None, "head", None),
            P(None, "head", None),
            P(None, "ctx", None),
            P(None, "ctx", None),
            P(),
            P("head", None, "ctx"),
            P("head", None, None),
            P("head", "ctx"),
        ),
        out_specs=P("head", "ctx"),
        check_vma=False,
    )
```
